128 devices in a mesh: view: 32 (over x, y, core), row: 4 (over z).
Axes of the slice: x: 4, y: 4, z: 4, core: 2. Of those that a mesh axis runs over, the one named last changes fastest.
Arguments:
- views_x: bfloat16 [32, 2048, 512], P('view', 'row'), may hold values from -17 to 17
- dy: bfloat16 [32, 2048, 512], P('view', 'row'), may hold values from -6 to 6
- w_query: bfloat16 [512, 512], replicated, may hold values from -0.25 to 0.25
- w_key: bfloat16 [512, 512], replicated, may hold values from -0.25 to 0.25
- w_value: bfloat16 [512, 512], replicated, may hold values from -0.25 to 0.25
- w_out: bfloat16 [512, 512], replicated, may hold values from -0.25 to 0.25
- key_lists: int32 [512, 32], replicated, may hold values from 0 to 2047, as said below
- key_counts: int32 [512], replicated, may hold values from 2 to 32
Outputs:
- grad_x: bfloat16 [32, 2048, 512], P('view', 'row')
- grad_w_out: float32 [512, 512], replicated
The draws below stay inside these ranges and needn't reach their ends.
Inputs may be any that keep to these rules, and one draw needn't show every extreme that they name: `key_lists`: entry j of query block b names a key segment for j < key_counts[b] and is 0 from there on. The live entries of one list differ, and all lie in views other than the query block's. All query blocks of one device (its 4 blocks) name at most one segment of any one device (a device holds 16 segments).
All inputs are finite; a program needn't handle non-finite values.
Results may differ from the reference program's by a relative error of at most 0.03.
The reference program's roundings to bfloat16 on the way count: a program that leaves them out, or rounds other values in their place, can miss the bound.
Values may be sent and summed in bfloat16 or wider, within the bound.
No kernel may reach another device: no remote copies, remote signals or barrier semaphores. Data moves between devices by JAX's collectives and lax.ppermute only.
A program may use at most 128 MiB of HBM per device.

```python
import jax
import jax.numpy as jnp
from jax import lax

WIDTH = 512
HEADS = 8
HEAD_DIM = 64
QUERY_BLOCK = 128
KEY_SEG = 32
MAXK = 32
DEVS = 128
VIEWS = 32
VIEW_TOKENS = 2048
QB_DEV = 4
SEG_DEV = 16
NQB = 512


def draw_views_x(key, part):
    shape_all = (VIEWS, VIEW_TOKENS, WIDTH)
    base_key = jax.random.fold_in(key, 0)
    return jnp.clip(jax.random.normal(base_key, shape_all, jnp.float32), -4.0, 4.0).astype(jnp.bfloat16)


def lists_and_counts(key):
    base_key = jax.random.fold_in(key, 7)
    pair_key, level_key, full_key, count_key, perm_key, cover_key = jax.random.split(base_key, 6)
    band_size = DEVS // VIEWS
    others = DEVS - band_size
    pair_seg = jax.random.randint(pair_key, (DEVS, DEVS), 0, SEG_DEV)
    pair_seg = pair_seg.at[:, DEVS - 1].set(SEG_DEV - 1)
    level_bits = jax.random.randint(level_key, (DEVS,), 2, 6)
    high_count = jnp.minimum(jnp.left_shift(jnp.int32(1), level_bits), others)
    full_device = jax.random.randint(full_key, (), 0, DEVS - band_size)
    block_ids = jnp.arange(NQB, dtype=jnp.int32)
    dev_of = block_ids // QB_DEV
    raw_count = jax.random.randint(count_key, (NQB,), 0, 1 << 20)
    counts = 2 + raw_count % (high_count[dev_of] - 1)
    forced_block = (full_device + 1) % DEVS * QB_DEV
    counts = jnp.where(block_ids == forced_block, min(MAXK, others), counts)
    permuted = jax.vmap(lambda one_key: jax.random.permutation(one_key, others))(jax.random.split(perm_key, NQB))
    slot_index = jnp.arange(MAXK, dtype=jnp.int32)
    pick_cols = jnp.broadcast_to(jnp.clip(slot_index, 0, others - 1)[None, :], (NQB, MAXK))
    drawn_other = jnp.take_along_axis(permuted, pick_cols, axis=1)
    cover_perm = jax.random.permutation(cover_key, others)
    pos_full = slot_index[None, :] * QB_DEV + (block_ids % QB_DEV)[:, None]
    full_valid = pos_full < others
    full_other = cover_perm[jnp.clip(pos_full, 0, others - 1)]
    count_full = jnp.sum(full_valid.astype(jnp.int32), axis=1)
    is_full = dev_of == full_device
    counts = jnp.where(is_full, count_full, counts)
    other_index = jnp.where(is_full[:, None], full_other, drawn_other)
    view_start = dev_of // band_size * band_size
    source = jnp.where(other_index >= view_start[:, None], other_index + band_size, other_index)
    segment = pair_seg[dev_of[:, None], source]
    entry_id = source * SEG_DEV + segment
    is_live = slot_index[None, :] < counts[:, None]
    list_ids = jnp.where(is_live, entry_id, 0)
    return (list_ids.astype(jnp.int32), counts.astype(jnp.int32))


def draw_key_lists(key, part):
    return lists_and_counts(key)[0]


def draw_key_counts(key, part):
    return lists_and_counts(key)[1]


def block_scale(key, dims, cuts, smallest, largest):
    loudness, own = 1.0, jax.random.fold_in(key, 6)
    for dim, shards_of in cuts:
        draws = jnp.exp(jax.random.uniform(jax.random.fold_in(own, dim), (shards_of,), jnp.float32, smallest / len(cuts), largest / len(cuts)))
        loudness = loudness * jnp.repeat(draws, dims[dim] // shards_of).reshape([-1 if axis == dim else 1 for axis in range(len(dims))])
    return loudness


def noise(key, dims, deviation, limit, cuts=(), held_as=jnp.bfloat16):
    factor_of = block_scale(key, dims, cuts, -0.22, 0.18) if cuts else 1.0
    array = jax.random.normal(key, dims, jnp.float32) * deviation * factor_of
    return jnp.minimum(jnp.maximum(array, -limit), limit).astype(held_as)


def setup_inputs(seed: int = 0) -> dict:
    keys = jax.random.split(jax.random.key(seed), 9)
    return {
        "views_x": draw_views_x(jax.random.fold_in(keys[8], 71), 0),
        "dy": noise(keys[1], (VIEWS, VIEW_TOKENS, WIDTH), 1.0, 6.0, ((0, 32), (1, 4))),
        "w_query": noise(keys[2], (WIDTH, WIDTH), WIDTH ** -0.5, 0.25),
        "w_key": noise(keys[3], (WIDTH, WIDTH), WIDTH ** -0.5, 0.25),
        "w_value": noise(keys[4], (WIDTH, WIDTH), WIDTH ** -0.5, 0.25),
        "w_out": noise(keys[5], (WIDTH, WIDTH), WIDTH ** -0.5, 0.25),
        "key_lists": draw_key_lists(jax.random.fold_in(keys[8], 71), 0),
        "key_counts": draw_key_counts(jax.random.fold_in(keys[8], 71), 0),
    }


def attend(query_blk, grad_blk, key_blk, value_blk, is_live, w_key, w_value):
    blocks = query_blk.shape[0]
    score_scale = HEAD_DIM ** -0.5
    q_heads = query_blk.astype(jnp.float32).reshape(blocks, QUERY_BLOCK, HEADS, HEAD_DIM)
    g_heads = grad_blk.astype(jnp.float32).reshape(blocks, QUERY_BLOCK, HEADS, HEAD_DIM)
    k_heads = key_blk.astype(jnp.float32).reshape(blocks, -1, HEADS, HEAD_DIM)
    v_heads = value_blk.astype(jnp.float32).reshape(blocks, -1, HEADS, HEAD_DIM)
    scores = jnp.einsum('bqhd,bkhd->bhqk', q_heads, k_heads) * score_scale
    scores = jnp.where(is_live[:, None, None, :], scores, jnp.float32(-1e30))
    row_max = jnp.max(scores, axis=-1, keepdims=True)
    weights = jnp.exp(scores - row_max)
    weights = weights / jnp.sum(weights, axis=-1, keepdims=True)
    weights_low = weights.astype(jnp.bfloat16)
    attended = jnp.einsum('bhqk,bkhd->bqhd', weights_low.astype(jnp.float32), v_heads).astype(jnp.bfloat16)
    dweights = jnp.einsum('bqhd,bkhd->bhqk', g_heads, v_heads)
    row_delta = jnp.einsum('bqhd,bqhd->bhq', g_heads, attended.astype(jnp.float32))
    dscores = (weights * (dweights - row_delta[..., None])).astype(jnp.bfloat16)
    dquery = (jnp.einsum('bhqk,bkhd->bqhd', dscores.astype(jnp.float32), k_heads) * score_scale).astype(jnp.bfloat16)
    key_grad = (jnp.einsum('bhqk,bqhd->bkhd', dscores.astype(jnp.float32), q_heads) * score_scale).astype(jnp.bfloat16)
    dvalue = jnp.einsum('bhqk,bqhd->bkhd', weights_low.astype(jnp.float32), g_heads).astype(jnp.bfloat16)
    back_term = jnp.dot(key_grad.reshape(-1, WIDTH), w_key.T, preferred_element_type=jnp.float32)
    back_term = back_term + jnp.dot(dvalue.reshape(-1, WIDTH), w_value.T, preferred_element_type=jnp.float32)
    return attended.reshape(blocks * QUERY_BLOCK, WIDTH), dquery.reshape(blocks * QUERY_BLOCK, WIDTH), back_term


def reference(views_x, dy, w_query, w_key, w_value, w_out, key_lists, key_counts):
    token_rows = views_x.reshape(-1, WIDTH)
    grad_rows = dy.reshape(-1, WIDTH)
    queries = jnp.dot(token_rows, w_query, preferred_element_type=jnp.float32).astype(jnp.bfloat16)
    key_rows = jnp.dot(token_rows, w_key, preferred_element_type=jnp.float32).astype(jnp.bfloat16)
    value_rows = jnp.dot(token_rows, w_value, preferred_element_type=jnp.float32).astype(jnp.bfloat16)
    grad_out = jnp.dot(grad_rows, w_out.T, preferred_element_type=jnp.float32).astype(jnp.bfloat16)
    key_segs = key_rows.reshape(-1, KEY_SEG, WIDTH)
    value_segs = value_rows.reshape(-1, KEY_SEG, WIDTH)
    query_dev = queries.reshape(DEVS, QB_DEV, QUERY_BLOCK, WIDTH)
    grad_dev = grad_out.reshape(DEVS, QB_DEV, QUERY_BLOCK, WIDTH)
    lists_dev = key_lists.reshape(DEVS, QB_DEV, MAXK)
    counts_dev = key_counts.reshape(DEVS, QB_DEV)
    columns = jnp.arange(MAXK, dtype=jnp.int32)

    def device_step(carry_sum, device_item):
        query_blk, grad_blk, list_blk, count_blk = device_item
        key_blk = key_segs[list_blk].reshape(QB_DEV, MAXK * KEY_SEG, WIDTH)
        value_blk = value_segs[list_blk].reshape(QB_DEV, MAXK * KEY_SEG, WIDTH)
        is_live = jnp.repeat(columns[None, :] < count_blk[:, None], KEY_SEG, axis=1)
        attended, dquery, back_term = attend(query_blk, grad_blk, key_blk, value_blk, is_live, w_key, w_value)
        carry_sum = carry_sum.at[list_blk.reshape(-1)].add(back_term.reshape(-1, KEY_SEG, WIDTH))
        return carry_sum, (attended, dquery)

    start_sum = jnp.zeros((DEVS * SEG_DEV, KEY_SEG, WIDTH), jnp.float32)
    carry_sum, (attended_all, dquery_all) = lax.scan(device_step, start_sum, (query_dev, grad_dev, lists_dev, counts_dev))
    attended_all = attended_all.reshape(-1, WIDTH)
    dquery_all = dquery_all.reshape(-1, WIDTH)
    query_part = jnp.dot(dquery_all, w_query.T, preferred_element_type=jnp.float32)
    grad_x = (query_part + carry_sum.reshape(-1, WIDTH)).astype(jnp.bfloat16).reshape(views_x.shape)
    grad_w_out = lax.dot_general(attended_all, grad_rows, (((0,), (0,)), ((), ())), preferred_element_type=jnp.float32)
    return grad_x, grad_w_out
```

```python
import functools

import jax
import jax.numpy as jnp
from jax import lax
from jax.experimental import pallas as pl
from jax.experimental.pallas import tpu as pltpu
from jax.sharding import PartitionSpec as P

HEADS = 8
HEAD_DIM = 64
QUERY_BLOCK = 128
KEY_SEG = 32
MAXK = 32
AXES = ("view", "row")
SPAN = MAXK * KEY_SEG
CHUNK = 256
PAIR = 2 * HEAD_DIM
MIB = 1024 * 1024
F32 = jnp.float32
BF16 = jnp.bfloat16


def dot(a, b, ca=1, cb=0):
    return lax.dot_general(a, b, (((ca,), (cb,)), ((), ())), preferred_element_type=F32)


def gather_kernel(wanted, x_ref, out_ref):
    def step(i, carry):
        out_ref[i] = x_ref[jnp.maximum(wanted[i], 0)]
        return carry

    lax.fori_loop(0, out_ref.shape[0], step, 0, unroll=8)


def combine_kernel(wanted, back_ref, base_ref, out_ref, acc_ref):
    acc_ref[...] = base_ref[...]

    def step(i, carry):
        seg = wanted[i]

        @pl.when(seg >= 0)
        def _():
            acc_ref[seg] += back_ref[i].astype(F32)

        return carry

    lax.fori_loop(0, back_ref.shape[0], step, 0, unroll=4)
    out_ref[...] = acc_ref[...].astype(out_ref.dtype)


def attention_kernel(
    sources, counts, x_ref, q_ref, g_ref, gt_ref, wk_ref, wv_ref,
    ret_ref, att_ref, dq_ref,
    xg, ks, vs, ss, ps, ds, dk, dv, acc,
):
    blocks = q_ref.shape[0] // QUERY_BLOCK
    width = x_ref.shape[-1]
    pairs = width // PAIR
    acc[...] = jnp.zeros_like(acc)
    lane = lax.broadcasted_iota(jnp.int32, (QUERY_BLOCK, PAIR), 1)
    low_half = lane < HEAD_DIM
    row_ids = lax.broadcasted_iota(jnp.int32, (CHUNK, 2 * QUERY_BLOCK), 0)
    chunks = SPAN // CHUNK

    def split_heads(rows):
        zero = jnp.zeros_like(rows)
        return jnp.concatenate(
            [jnp.where(low_half, rows, zero), jnp.where(low_half, zero, rows)], axis=0
        )

    def fold(rows, op):
        return op(rows.reshape(CHUNK // 8, 8, rows.shape[-1]), axis=0)

    def block_step(b, carry):
        tok = pl.ds(pl.multiple_of(b * QUERY_BLOCK, QUERY_BLOCK), QUERY_BLOCK)
        live_rows = counts[b] * KEY_SEG
        for j in range(MAXK):
            xg[pl.ds(j * KEY_SEG, KEY_SEG), :] = x_ref[sources[b * MAXK + j]]
        for c in range(chunks):
            rows = pl.ds(c * CHUNK, CHUNK)
            part = xg[rows, :]
            ks[rows, :] = dot(part, wk_ref[...]).astype(BF16)
            vs[rows, :] = dot(part, wv_ref[...]).astype(BF16)
        for p in range(pairs):
            cols = pl.ds(p * PAIR, PAIR)
            qb = split_heads(q_ref[tok, cols])
            gb = split_heads(g_ref[tok, cols])
            top = jnp.full((8, 2 * QUERY_BLOCK), -1e30, F32)
            for c in range(chunks):
                rows = pl.ds(c * CHUNK, CHUNK)
                s = dot(ks[rows, cols], qb, 1, 1)
                s = jnp.where(row_ids < live_rows - c * CHUNK, s, F32(-1e30))
                ss[rows, :] = s
                top = jnp.maximum(top, fold(s, jnp.max))
            top = jnp.max(top, axis=0, keepdims=True)
            total = jnp.zeros((8, 2 * QUERY_BLOCK), F32)
            for c in range(chunks):
                rows = pl.ds(c * CHUNK, CHUNK)
                e = jnp.exp(ss[rows, :] - top)
                ss[rows, :] = e
                total = total + fold(e, jnp.sum)
            inverse = 1.0 / jnp.sum(total, axis=0, keepdims=True)
            for c in range(chunks):
                rows = pl.ds(c * CHUNK, CHUNK)
                w = ss[rows, :] * inverse
                ss[rows, :] = w
                low = w.astype(BF16)
                ps[rows, :] = low
                dv[rows, cols] = dot(low, gb).astype(BF16)
            att = dot(vs[:, cols], ps[...], 0, 0)
            deltas = []
            for h in range(2):
                here = att[h * HEAD_DIM:(h + 1) * HEAD_DIM, h * QUERY_BLOCK:(h + 1) * QUERY_BLOCK]
                here = here.astype(BF16)
                chan = pl.ds(p * PAIR + h * HEAD_DIM, HEAD_DIM)
                att_ref[chan, tok] = here
                both = here.astype(F32) * gt_ref[chan, tok].astype(F32)
                deltas.append(jnp.sum(both, axis=0, keepdims=True))
            delta = jnp.concatenate(deltas, axis=1)
            for c in range(chunks):
                rows = pl.ds(c * CHUNK, CHUNK)
                dp = dot(vs[rows, cols], gb, 1, 1)
                low = (ss[rows, :] * (dp - delta)).astype(BF16)
                ds[rows, :] = low
                dk[rows, cols] = dot(low, qb).astype(BF16)
            dq = dot(ks[:, cols], ds[...], 0, 0) * F32(HEAD_DIM ** -0.5)
            for h in range(2):
                here = dq[h * HEAD_DIM:(h + 1) * HEAD_DIM, h * QUERY_BLOCK:(h + 1) * QUERY_BLOCK]
                dq_ref[pl.ds(p * PAIR + h * HEAD_DIM, HEAD_DIM), tok] = here.astype(BF16)
        for c in range(chunks):
            rows = pl.ds(c * CHUNK, CHUNK)
            term = dot(dk[rows, :], wk_ref[...], 1, 1) + dot(dv[rows, :], wv_ref[...], 1, 1)
            per = CHUNK // KEY_SEG
            for j in range(per):
                acc[sources[b * MAXK + c * per + j]] += term[j * KEY_SEG:(j + 1) * KEY_SEG, :]
        return carry

    lax.fori_loop(0, blocks, block_step, 0)
    ret_ref[...] = acc[...].astype(BF16)


VMEM = pl.BlockSpec(memory_space=pltpu.VMEM)
SMEM = pl.BlockSpec(memory_space=pltpu.SMEM)


def exchange(v):
    return lax.all_to_all(v, AXES, split_axis=0, concat_axis=0, tiled=True)


def local(views_x, dy, w_query, w_key, w_value, w_out, key_lists, key_counts):
    width = views_x.shape[-1]
    x = views_x.reshape(-1, width)
    grads = dy.reshape(-1, width)
    tokens = x.shape[0]
    devices = lax.axis_size(AXES)
    me = lax.axis_index(AXES)
    seg_dev = tokens // KEY_SEG
    blocks = tokens // QUERY_BLOCK
    columns = jnp.arange(MAXK, dtype=jnp.int32)
    live = columns[None, :] < key_counts[:, None]
    asked = live & (key_lists // seg_dev == me)
    wanted = jnp.max(
        jnp.where(asked, key_lists % seg_dev, -1).reshape(devices, blocks * MAXK), axis=1
    )
    outgoing = pl.pallas_call(
        gather_kernel,
        out_shape=jax.ShapeDtypeStruct((devices, KEY_SEG, width), BF16),
        in_specs=[SMEM, VMEM],
        out_specs=VMEM,
        compiler_params=pltpu.CompilerParams(vmem_limit_bytes=16 * MIB),
        name="gather",
    )(wanted, x.reshape(seg_dev, KEY_SEG, width))
    fetched = exchange(outgoing)

    queries = dot(x, w_query).astype(BF16) * BF16(HEAD_DIM ** -0.5)
    grad_out = dot(grads, w_out, 1, 1).astype(BF16)
    grad_out_t = grad_out.T
    sources = lax.dynamic_slice_in_dim(key_lists, me * blocks, blocks, 0).reshape(-1) // seg_dev
    counts = lax.dynamic_slice_in_dim(key_counts, me * blocks, blocks, 0)
    pair2 = 2 * QUERY_BLOCK
    ret, att_t, dq_t = pl.pallas_call(
        attention_kernel,
        out_shape=[
            jax.ShapeDtypeStruct((devices, KEY_SEG, width), BF16),
            jax.ShapeDtypeStruct((width, tokens), BF16),
            jax.ShapeDtypeStruct((width, tokens), BF16),
        ],
        in_specs=[SMEM, SMEM] + [VMEM] * 6,
        out_specs=[VMEM] * 3,
        scratch_shapes=[
            pltpu.VMEM((SPAN, width), BF16),
            pltpu.VMEM((SPAN, width), BF16),
            pltpu.VMEM((SPAN, width), BF16),
            pltpu.VMEM((SPAN, pair2), F32),
            pltpu.VMEM((SPAN, pair2), BF16),
            pltpu.VMEM((SPAN, pair2), BF16),
            pltpu.VMEM((SPAN, width), BF16),
            pltpu.VMEM((SPAN, width), BF16),
            pltpu.VMEM((devices, KEY_SEG, width), F32),
        ],
        compiler_params=pltpu.CompilerParams(vmem_limit_bytes=48 * MIB),
        name="attention",
    )(sources, counts, fetched, queries, grad_out, grad_out_t, w_key, w_value)

    local_grad = dot(att_t, grads).astype(BF16)
    part = exchange(local_grad.reshape(devices, width // devices, width))
    part = jnp.sum(part.astype(F32), axis=0)
    grad_w_out = exchange(jnp.broadcast_to(part, (devices,) + part.shape)).reshape(width, width)

    back = exchange(ret)
    base = dot(dq_t, w_query, 0, 1)
    grad_x = pl.pallas_call(
        combine_kernel,
        out_shape=jax.ShapeDtypeStruct((seg_dev, KEY_SEG, width), BF16),
        in_specs=[SMEM, VMEM, VMEM],
        out_specs=VMEM,
        scratch_shapes=[pltpu.VMEM((seg_dev, KEY_SEG, width), F32)],
        compiler_params=pltpu.CompilerParams(vmem_limit_bytes=16 * MIB),
        name="combine",
    )(wanted, back, base.reshape(seg_dev, KEY_SEG, width))
    return grad_x.reshape(views_x.shape), grad_w_out


def solution(mesh):
    in_specs = (P("view", "row", None), P("view", "row", None), P(), P(), P(), P(), P(), P())
    out_specs = (P("view", "row", None), P())
    return jax.shard_map(local, mesh=mesh, in_specs=in_specs, out_specs=out_specs, check_vma=False)
```

```python
import jax
import jax.numpy as jnp
from jax import lax
from jax.experimental import pallas as pl
from jax.experimental.pallas import tpu as pltpu
from jax.sharding import PartitionSpec as P

HEADS = 8
HEAD_DIM = 64
QUERY_BLOCK = 128
KEY_SEG = 32
MAXK = 32
AXES = ("view", "row")
SPAN = MAXK * KEY_SEG
CHUNK = 256
PAIR = 2 * HEAD_DIM
BOTH = 2 * QUERY_BLOCK
LANES = 128
MIB = 1024 * 1024
F32 = jnp.float32
BF16 = jnp.bfloat16


def dot(a, b, ca=1, cb=0):
    return lax.dot_general(a, b, (((ca,), (cb,)), ((), ())), preferred_element_type=F32)


def gather_kernel(wanted, x_ref, out_ref):
    def step(i, carry):
        out_ref[i] = x_ref[jnp.maximum(wanted[i], 0)]
        return carry

    lax.fori_loop(0, out_ref.shape[0], step, 0, unroll=8)


def combine_kernel(wanted, back_ref, base_ref, out_ref, acc_ref):
    acc_ref[...] = base_ref[...]

    def step(i, carry):
        seg = wanted[i]

        @pl.when(seg >= 0)
        def _():
            acc_ref[seg] += back_ref[i].astype(F32)

        return carry

    lax.fori_loop(0, back_ref.shape[0], step, 0, unroll=4)
    out_ref[...] = acc_ref[...].astype(out_ref.dtype)


def split_heads(rows):
    low_half = lax.broadcasted_iota(jnp.int32, rows.shape, 1) < HEAD_DIM
    zero = jnp.zeros_like(rows)
    return jnp.concatenate(
        [jnp.where(low_half, rows, zero), jnp.where(low_half, zero, rows)], axis=0
    )


def fold(rows, op):
    return op(rows.reshape(rows.shape[0] // 8, 8, rows.shape[-1]), axis=0)


def token_rows(b):
    return pl.ds(pl.multiple_of(b * QUERY_BLOCK, QUERY_BLOCK), QUERY_BLOCK)


def masked_scores(k_rows, qb, live_rows, start):
    s = dot(k_rows, qb, 1, 1)
    ids = lax.broadcasted_iota(jnp.int32, s.shape, 0)
    return jnp.where(ids < live_rows - start, s, F32(-1e30))


def forward_kernel(
    sources, counts, x_ref, q_ref, gt_ref, wk_ref, wv_ref, dy_ref,
    k_ref, v_ref, stat_ref, grad_ref,
    xg, ss, ps, att, sems,
):
    blocks = q_ref.shape[0] // QUERY_BLOCK
    width = x_ref.shape[-1]
    pairs = width // PAIR

    def fetch(b):
        def one(j, carry):
            pltpu.make_async_copy(
                x_ref.at[sources[b * MAXK + j]], xg.at[b * MAXK + j], sems.at[b]
            ).start()
            return carry

        lax.fori_loop(0, MAXK, one, 0, unroll=8)

    fetch(0)

    def block_step(b, carry):
        @pl.when(b + 1 < blocks)
        def _():
            fetch(b + 1)

        mine = xg.at[pl.ds(b * MAXK, MAXK)]
        pltpu.make_async_copy(mine, mine, sems.at[b]).wait()
        tok = token_rows(b)
        live_rows = counts[b] * KEY_SEG
        base = pl.multiple_of(b * SPAN, SPAN)
        segs = CHUNK // KEY_SEG
        for c in range(SPAN // CHUNK):
            rows = pl.ds(base + c * CHUNK, CHUNK)
            part = xg[pl.ds(b * MAXK + c * segs, segs)].reshape(CHUNK, width)
            k_ref[rows, :] = dot(part, wk_ref[...]).astype(BF16)
            v_ref[rows, :] = dot(part, wv_ref[...]).astype(BF16)
        for p in range(pairs):
            cols = pl.ds(p * PAIR, PAIR)
            qb = split_heads(q_ref[tok, cols])
            top = jnp.full((8, BOTH), -1e30, F32)
            for c in range(SPAN // CHUNK):
                rows = pl.ds(c * CHUNK, CHUNK)
                s = masked_scores(
                    k_ref[pl.ds(base + c * CHUNK, CHUNK), cols], qb, live_rows, c * CHUNK
                )
                ss[p % 2, rows, :] = s
                top = jnp.maximum(top, fold(s, jnp.max))
            top = jnp.max(top, axis=0, keepdims=True)
            total = jnp.zeros((8, BOTH), F32)
            for c in range(SPAN // CHUNK):
                rows = pl.ds(c * CHUNK, CHUNK)
                e = jnp.exp(ss[p % 2, rows, :] - top)
                ss[p % 2, rows, :] = e
                total = total + fold(e, jnp.sum)
            total = jnp.sum(total, axis=0, keepdims=True)
            inverse = 1.0 / total
            for c in range(SPAN // CHUNK):
                rows = pl.ds(c * CHUNK, CHUNK)
                ps[p % 2, rows, :] = (ss[p % 2, rows, :] * inverse).astype(BF16)
            out = dot(v_ref[pl.ds(base, SPAN), cols], ps[p % 2], 0, 0)
            deltas = []
            for h in range(2):
                here = out[h * HEAD_DIM:(h + 1) * HEAD_DIM, h * QUERY_BLOCK:(h + 1) * QUERY_BLOCK]
                here = here.astype(BF16)
                chan = pl.ds(p * PAIR + h * HEAD_DIM, HEAD_DIM)
                att[chan, tok] = here
                both = here.astype(F32) * gt_ref[chan, tok].astype(F32)
                deltas.append(jnp.sum(both, axis=0, keepdims=True))
            stat_ref[b, pl.ds(p, 1), :] = top + jnp.log(total)
            stat_ref[b, pl.ds(pairs + p, 1), :] = jnp.concatenate(deltas, axis=1)
        return carry

    lax.fori_loop(0, blocks, block_step, 0)
    per = grad_ref.shape[1]
    slots = width // LANES
    for r in range(width // 128):
        g = dot(att[pl.ds(r * 128, 128), :], dy_ref[...]).astype(BF16)
        for i in range(128 // per):
            for t in range(slots):
                grad_ref[(r * (128 // per) + i) * slots + t] = g[
                    i * per:(i + 1) * per, t * LANES:(t + 1) * LANES
                ]


def backward_kernel(
    sources, counts, k_ref, v_ref, q_ref, g_ref, stat_ref, wk_ref, wv_ref,
    ret_ref, dq_ref,
    ds, dk, dv, acc,
):
    blocks = q_ref.shape[0] // QUERY_BLOCK
    width = wk_ref.shape[-1]
    pairs = width // PAIR
    segs = CHUNK // KEY_SEG
    acc[...] = jnp.zeros_like(acc)

    def block_step(b, carry):
        tok = token_rows(b)
        live_rows = counts[b] * KEY_SEG
        base = pl.multiple_of(b * SPAN, SPAN)
        for p in range(pairs):
            cols = pl.ds(p * PAIR, PAIR)
            qb = split_heads(q_ref[tok, cols])
            gb = split_heads(g_ref[tok, cols])
            lse = stat_ref[b, pl.ds(p, 1), :]
            delta = stat_ref[b, pl.ds(pairs + p, 1), :]
            for c in range(SPAN // CHUNK):
                rows = pl.ds(c * CHUNK, CHUNK)
                there = pl.ds(base + c * CHUNK, CHUNK)
                s = masked_scores(k_ref[there, cols], qb, live_rows, c * CHUNK)
                w = jnp.exp(s - lse)
                dv[rows, cols] = dot(w.astype(BF16), gb).astype(BF16)
                dp = dot(v_ref[there, cols], gb, 1, 1)
                low = (w * (dp - delta)).astype(BF16)
                ds[p % 2, rows, :] = low
                dk[rows, cols] = dot(low, qb).astype(BF16)
            dq = dot(k_ref[pl.ds(base, SPAN), cols], ds[p % 2], 0, 0) * F32(HEAD_DIM ** -0.5)
            for h in range(2):
                here = dq[h * HEAD_DIM:(h + 1) * HEAD_DIM, h * QUERY_BLOCK:(h + 1) * QUERY_BLOCK]
                dq_ref[pl.ds(p * PAIR + h * HEAD_DIM, HEAD_DIM), tok] = here.astype(BF16)
        for c in range(SPAN // CHUNK):
            rows = pl.ds(c * CHUNK, CHUNK)
            term = dot(dk[rows, :], wk_ref[...], 1, 1) + dot(dv[rows, :], wv_ref[...], 1, 1)
            for j in range(segs):
                acc[sources[b * MAXK + c * segs + j]] += term[j * KEY_SEG:(j + 1) * KEY_SEG, :]
        return carry

    lax.fori_loop(0, blocks, block_step, 0)
    ret_ref[...] = acc[...].astype(BF16)


VMEM = pl.BlockSpec(memory_space=pltpu.VMEM)
SMEM = pl.BlockSpec(memory_space=pltpu.SMEM)
ANY = pl.BlockSpec(memory_space=pl.ANY)


def exchange(v):
    return lax.all_to_all(v, AXES, split_axis=0, concat_axis=0, tiled=True)


def forward(sources, counts, fetched, queries, grad_out_t, w_key, w_value, grads):
    devices, _, width = fetched.shape
    tokens = queries.shape[0]
    blocks = tokens // QUERY_BLOCK
    keys = blocks * SPAN
    per = width * width // (devices * LANES)
    return pl.pallas_call(
        forward_kernel,
        out_shape=[
            jax.ShapeDtypeStruct((keys, width), BF16),
            jax.ShapeDtypeStruct((keys, width), BF16),
            jax.ShapeDtypeStruct((blocks, 2 * width // PAIR, BOTH), F32),
            jax.ShapeDtypeStruct((devices, per, LANES), BF16),
        ],
        in_specs=[SMEM, SMEM, ANY] + [VMEM] * 5,
        out_specs=[VMEM] * 4,
        scratch_shapes=[
            pltpu.VMEM((blocks * MAXK, KEY_SEG, width), BF16),
            pltpu.VMEM((2, SPAN, BOTH), F32),
            pltpu.VMEM((2, SPAN, BOTH), BF16),
            pltpu.VMEM((width, tokens), BF16),
            pltpu.SemaphoreType.DMA((blocks,)),
        ],
        compiler_params=pltpu.CompilerParams(vmem_limit_bytes=32 * MIB),
        cost_estimate=pl.CostEstimate(
            flops=10_000_000_000, bytes_accessed=8 * MIB, transcendentals=4 * MIB
        ),
        name="forward",
    )(sources, counts, fetched, queries, grad_out_t, w_key, w_value, grads)


def backward(sources, counts, keys, values, queries, grad_out, stats, w_key, w_value, devices):
    tokens, width = queries.shape
    return pl.pallas_call(
        backward_kernel,
        out_shape=[
            jax.ShapeDtypeStruct((devices, KEY_SEG, width), BF16),
            jax.ShapeDtypeStruct((width, tokens), BF16),
        ],
        in_specs=[SMEM, SMEM] + [VMEM] * 7,
        out_specs=[VMEM] * 2,
        scratch_shapes=[
            pltpu.VMEM((2, SPAN, BOTH), BF16),
            pltpu.VMEM((SPAN, width), BF16),
            pltpu.VMEM((SPAN, width), BF16),
            pltpu.VMEM((devices, KEY_SEG, width), F32),
        ],
        compiler_params=pltpu.CompilerParams(vmem_limit_bytes=32 * MIB),
        cost_estimate=pl.CostEstimate(
            flops=20_000_000_000, bytes_accessed=16 * MIB, transcendentals=4 * MIB
        ),
        name="backward",
    )(sources, counts, keys, values, queries, grad_out, stats, w_key, w_value)


def local(views_x, dy, w_query, w_key, w_value, w_out, key_lists, key_counts):
    width = views_x.shape[-1]
    x = views_x.reshape(-1, width)
    grads = dy.reshape(-1, width)
    tokens = x.shape[0]
    devices = lax.axis_size(AXES)
    me = lax.axis_index(AXES)
    seg_dev = tokens // KEY_SEG
    blocks = tokens // QUERY_BLOCK
    columns = jnp.arange(MAXK, dtype=jnp.int32)
    live = columns[None, :] < key_counts[:, None]
    asked = live & (key_lists // seg_dev == me)
    wanted = jnp.max(
        jnp.where(asked, key_lists % seg_dev, -1).reshape(devices, blocks * MAXK), axis=1
    )
    outgoing = pl.pallas_call(
        gather_kernel,
        out_shape=jax.ShapeDtypeStruct((devices, KEY_SEG, width), BF16),
        in_specs=[SMEM, VMEM],
        out_specs=VMEM,
        compiler_params=pltpu.CompilerParams(vmem_limit_bytes=16 * MIB),
        name="gather",
    )(wanted, x.reshape(seg_dev, KEY_SEG, width))
    fetched = exchange(outgoing)

    queries = dot(x, w_query).astype(BF16) * BF16(HEAD_DIM ** -0.5)
    grad_out = dot(grads, w_out, 1, 1).astype(BF16)
    grad_out_t = grad_out.T
    sources = lax.dynamic_slice_in_dim(key_lists, me * blocks, blocks, 0).reshape(-1) // seg_dev
    counts = lax.dynamic_slice_in_dim(key_counts, me * blocks, blocks, 0)
    keys, values, stats, pieces = forward(
        sources, counts, fetched, queries, grad_out_t, w_key, w_value, grads
    )
    parts = exchange(pieces)
    ret, dq_t = backward(
        sources, counts, keys, values, queries, grad_out, stats, w_key, w_value, devices
    )
    part = jnp.sum(parts.astype(F32), axis=0)
    whole = lax.all_gather(part, AXES, axis=0)
    rows = part.shape[0]
    slots = width // LANES
    grad_w_out = whole.reshape(width // rows, slots, rows, LANES).transpose(0, 2, 1, 3)
    grad_w_out = grad_w_out.reshape(width, width)

    back = exchange(ret)
    base = dot(dq_t, w_query, 0, 1)
    grad_x = pl.pallas_call(
        combine_kernel,
        out_shape=jax.ShapeDtypeStruct((seg_dev, KEY_SEG, width), BF16),
        in_specs=[SMEM, VMEM, VMEM],
        out_specs=VMEM,
        scratch_shapes=[pltpu.VMEM((seg_dev, KEY_SEG, width), F32)],
        compiler_params=pltpu.CompilerParams(vmem_limit_bytes=16 * MIB),
        name="combine",
    )(wanted, back, base.reshape(seg_dev, KEY_SEG, width))
    return grad_x.reshape(views_x.shape), grad_w_out


def solution(mesh):
    in_specs = (P("view", "row", None), P("view", "row", None), P(), P(), P(), P(), P(), P())
    out_specs = (P("view", "row", None), P())
    return jax.shard_map(local, mesh=mesh, in_specs=in_specs, out_specs=out_specs, check_vma=False)
```

```python
import jax
import jax.numpy as jnp
from jax import lax
from jax.experimental import pallas as pl
from jax.experimental.pallas import tpu as pltpu
from jax.sharding import PartitionSpec as P

HEAD_DIM = 64
QUERY_BLOCK = 128
KEY_SEG = 32
MAXK = 32
AXES = ("view", "row")
SPAN = MAXK * KEY_SEG
PAIR = 2 * HEAD_DIM
BOTH = 2 * QUERY_BLOCK
LANES = 128
MIB = 1024 * 1024
F32 = jnp.float32
BF16 = jnp.bfloat16
FC = 256
BC = 256
PC = 256
MXUMASK = False
NORM = False
ABL = ""

def dot(a, b, ca=1, cb=0):
    return lax.dot_general(a, b, (((ca,), (cb,)), ((), ())), preferred_element_type=F32)

def split_heads(rows):
    low_half = lax.broadcasted_iota(jnp.int32, rows.shape, 1) < HEAD_DIM
    zero = jnp.zeros_like(rows)
    return jnp.concatenate(
        [jnp.where(low_half, rows, zero), jnp.where(low_half, zero, rows)], axis=0)

def fold(rows, op):
    return op(rows.reshape(rows.shape[0] // 8, 8, rows.shape[-1]), axis=0)

def token_rows(b):
    return pl.ds(pl.multiple_of(b * QUERY_BLOCK, QUERY_BLOCK), QUERY_BLOCK)

def masked_scores(k_rows, qb, live_rows, start, bias=None):
    if MXUMASK:
        return dot(jnp.concatenate([k_rows, bias], axis=1), qb, 1, 1)
    s = dot(k_rows, qb, 1, 1)
    ids = lax.broadcasted_iota(jnp.int32, s.shape, 0)
    return jnp.where(ids < live_rows - start, s, F32(-1e30))

def with_ones(qb):
    if not MXUMASK:
        return qb
    lane = lax.broadcasted_iota(jnp.int32, (BOTH, LANES), 1)
    return jnp.concatenate([qb, jnp.where(lane == 0, 1.0, 0.0).astype(BF16)], axis=1)

def fill_bias(bias, live_rows):
    if MXUMASK:
        ids = lax.broadcasted_iota(jnp.int32, bias.shape, 0)
        lane = lax.broadcasted_iota(jnp.int32, bias.shape, 1)
        bias[...] = jnp.where((ids >= live_rows) & (lane == 0), F32(-1e30), F32(0)).astype(BF16)

def forward_kernel(
    sources, counts, x_hbm, q_hbm, gt_hbm, wk_hbm, wv_hbm, dy_hbm,
    k_out, v_out, stat_ref, grad_ref,
    xg, ks, vs, ss, ps, att, bias, q_ref, gt_ref, wk_ref, wv_ref, dy_ref, sems, osems, wsems,
):
    blocks = q_ref.shape[0] // QUERY_BLOCK
    width = x_hbm.shape[-1]
    pairs = width // PAIR

    def fetch(b):
        def one(j, carry):
            pltpu.make_async_copy(
                x_hbm.at[sources[b * MAXK + j]], xg.at[b * MAXK + j], sems.at[b]
            ).start()
            return carry
        lax.fori_loop(0, MAXK, one, 0, unroll=8)

    weights = [(wk_hbm, wk_ref), (wv_hbm, wv_ref), (q_hbm, q_ref), (gt_hbm, gt_ref), (dy_hbm, dy_ref)]
    loads = [pltpu.make_async_copy(a, z, wsems.at[i]) for i, (a, z) in enumerate(weights)]
    loads[0].start()
    loads[1].start()
    fetch(0)
    for load in loads[2:]:
        load.start()
    loads[0].wait()
    loads[1].wait()

    def block_step(b, carry):
        @pl.when(b + 1 < blocks)
        def _():
            fetch(b + 1)
        mine = xg.at[pl.ds(b * MAXK, MAXK)]
        pltpu.make_async_copy(mine, mine, sems.at[b]).wait()
        tok = token_rows(b)
        live_rows = counts[b] * KEY_SEG
        base = pl.multiple_of(b * SPAN, SPAN)
        segs = PC // KEY_SEG
        fill_bias(bias, live_rows)
        if "noproj" not in ABL:
            for c in range(SPAN // PC):
                rows = pl.ds(base + c * PC, PC)
                part = xg[pl.ds(b * MAXK + c * segs, segs)].reshape(PC, width)
                ks[rows, :] = dot(part, wk_ref[...]).astype(BF16)
                vs[rows, :] = dot(part, wv_ref[...]).astype(BF16)
        span = pl.ds(base, SPAN)
        pltpu.make_async_copy(ks.at[span], k_out.at[span], osems.at[0]).start()
        pltpu.make_async_copy(vs.at[span], v_out.at[span], osems.at[1]).start()

        @pl.when(b == 0)
        def _():
            for load in loads[2:]:
                load.wait()
        for p in range(pairs if "nopair" not in ABL else 0):
            cols = pl.ds(p * PAIR, PAIR)
            qb = with_ones(split_heads(q_ref[tok, cols]))
            top = jnp.full((8, BOTH), -1e30, F32)
            for c in range(SPAN // FC):
                rows = pl.ds(c * FC, FC)
                s = masked_scores(ks[pl.ds(base + c * FC, FC), cols], qb, live_rows, c * FC, bias[rows, :])
                ss[p % 2, rows, :] = s
                top = jnp.maximum(top, fold(s, jnp.max))
            top = jnp.max(top, axis=0, keepdims=True)
            total = jnp.zeros((8, BOTH), F32)
            for c in range(SPAN // FC):
                rows = pl.ds(c * FC, FC)
                e = jnp.exp(ss[p % 2, rows, :] - top)
                if NORM:
                    ss[p % 2, rows, :] = e
                else:
                    ps[p % 2, rows, :] = e.astype(BF16)
                total = total + fold(e, jnp.sum)
            total = jnp.sum(total, axis=0, keepdims=True)
            inverse = 1.0 / total
            if NORM:
                for c in range(SPAN // FC):
                    rows = pl.ds(c * FC, FC)
                    ps[p % 2, rows, :] = (ss[p % 2, rows, :] * inverse).astype(BF16)
            out = dot(vs[pl.ds(base, SPAN), cols], ps[p % 2], 0, 0)
            deltas = []
            for h in range(2):
                here = out[h * HEAD_DIM:(h + 1) * HEAD_DIM, h * QUERY_BLOCK:(h + 1) * QUERY_BLOCK]
                if not NORM:
                    here = here * inverse[:, h * QUERY_BLOCK:(h + 1) * QUERY_BLOCK]
                here = here.astype(BF16)
                chan = pl.ds(p * PAIR + h * HEAD_DIM, HEAD_DIM)
                att[chan, tok] = here
                both = here.astype(F32) * gt_ref[chan, tok].astype(F32)
                deltas.append(jnp.sum(both, axis=0, keepdims=True))
            stat_ref[b, pl.ds(p, 1), :] = top + jnp.log(total)
            stat_ref[b, pl.ds(pairs + p, 1), :] = jnp.concatenate(deltas, axis=1)
        return carry

    lax.fori_loop(0, blocks, block_step, 0)
    per = grad_ref.shape[1]
    slots = width // LANES
    for r in range(width // 128 if "nograd" not in ABL else 0):
        g = dot(att[pl.ds(r * 128, 128), :], dy_ref[...]).astype(BF16)
        for i in range(128 // per):
            for t in range(slots):
                grad_ref[(r * (128 // per) + i) * slots + t] = g[
                    i * per:(i + 1) * per, t * LANES:(t + 1) * LANES
                ]
    pltpu.make_async_copy(ks, k_out, osems.at[0]).wait()
    pltpu.make_async_copy(vs, v_out, osems.at[1]).wait()


def backward_kernel(
    sources, counts, k_hbm, v_hbm, q_hbm, g_hbm, stat_ref, wk_hbm, wv_hbm,
    ret_hbm, dq_ref,
    ks, vs, ds, dk, dv, acc, bias, q_ref, g_ref, wk_ref, wv_ref, out, sems, wsems, osem,
):
    blocks = q_ref.shape[0] // QUERY_BLOCK
    width = wk_ref.shape[-1]
    pairs = width // PAIR
    segs = PC // KEY_SEG
    devices = acc.shape[0]
    weights = [(q_hbm, q_ref), (g_hbm, g_ref), (wk_hbm, wk_ref), (wv_hbm, wv_ref)]
    loads = [pltpu.make_async_copy(a, z, wsems.at[i]) for i, (a, z) in enumerate(weights)]
    for load in loads[:2]:
        load.start()
    for b in range(blocks):
        span = pl.ds(b * SPAN, SPAN)
        pltpu.make_async_copy(k_hbm.at[span], ks.at[span], sems.at[b, 0]).start()
        pltpu.make_async_copy(v_hbm.at[span], vs.at[span], sems.at[b, 1]).start()
        if b == 0:
            for load in loads[2:]:
                load.start()
    acc[...] = jnp.zeros_like(acc)
    for load in loads:
        load.wait()

    def block_step(b, carry):
        tok = token_rows(b)
        live_rows = counts[b] * KEY_SEG
        base = pl.multiple_of(b * SPAN, SPAN)
        span = pl.ds(base, SPAN)
        fill_bias(bias, live_rows)
        pltpu.make_async_copy(ks.at[span], ks.at[span], sems.at[b, 0]).wait()
        pltpu.make_async_copy(vs.at[span], vs.at[span], sems.at[b, 1]).wait()
        for p in range(pairs if "nopair" not in ABL else 0):
            cols = pl.ds(p * PAIR, PAIR)
            qb = split_heads(q_ref[tok, cols])
            qo = with_ones(qb)
            gb = split_heads(g_ref[tok, cols])
            lse = stat_ref[b, pl.ds(p, 1), :]
            delta = stat_ref[b, pl.ds(pairs + p, 1), :]
            for c in range(SPAN // BC):
                rows = pl.ds(c * BC, BC)
                there = pl.ds(base + c * BC, BC)
                s = masked_scores(ks[there, cols], qo, live_rows, c * BC, bias[rows, :])
                w = jnp.exp(s - lse)
                dv[rows, cols] = dot(w.astype(BF16), gb).astype(BF16)
                dp = dot(vs[there, cols], gb, 1, 1)
                low = (w * (dp - delta)).astype(BF16)
                ds[p % 2, rows, :] = low
                dk[rows, cols] = dot(low, qb).astype(BF16)
            dq = dot(ks[pl.ds(base, SPAN), cols], ds[p % 2], 0, 0) * F32(HEAD_DIM ** -0.5)
            for h in range(2):
                here = dq[h * HEAD_DIM:(h + 1) * HEAD_DIM, h * QUERY_BLOCK:(h + 1) * QUERY_BLOCK]
                dq_ref[pl.ds(p * PAIR + h * HEAD_DIM, HEAD_DIM), tok] = here.astype(BF16)
        for c in range(SPAN // PC if "noproj" not in ABL else 0):
            rows = pl.ds(c * PC, PC)
            term = dot(dk[rows, :], wk_ref[...], 1, 1) + dot(dv[rows, :], wv_ref[...], 1, 1)
            for j in range(segs):
                acc[sources[b * MAXK + c * segs + j]] += term[j * KEY_SEG:(j + 1) * KEY_SEG, :]
        return carry

    lax.fori_loop(0, blocks, block_step, 0)
    groups = 4
    size = devices // groups
    for t in range(groups):
        part = pl.ds(t * size, size)
        for u in range(width // LANES):
            out[part, pl.ds(u * KEY_SEG, KEY_SEG), :] = acc[part, :, pl.ds(u * LANES, LANES)].astype(BF16)
        pltpu.make_async_copy(
            out.at[part], ret_hbm.at[part, pl.ds(0, KEY_SEG * width // LANES)], osem).start()
    pltpu.make_async_copy(out, ret_hbm.at[:, pl.ds(0, KEY_SEG * width // LANES)], osem).wait()


VMEM = pl.BlockSpec(memory_space=pltpu.VMEM)
SMEM = pl.BlockSpec(memory_space=pltpu.SMEM)
ANY = pl.BlockSpec(memory_space=pl.ANY)

def square(width, tokens):
    return pltpu.VMEM((tokens, width), BF16)

def forward(sources, counts, fetched, queries, grad_out_t, w_key, w_value, grads):
    devices, _, width = fetched.shape
    tokens = queries.shape[0]
    blocks = tokens // QUERY_BLOCK
    keys = blocks * SPAN
    per = width * width // (devices * LANES)
    return pl.pallas_call(
        forward_kernel,
        out_shape=[
            jax.ShapeDtypeStruct((keys, width), BF16),
            jax.ShapeDtypeStruct((keys, width), BF16),
            jax.ShapeDtypeStruct((blocks, 2 * width // PAIR, BOTH), F32),
            jax.ShapeDtypeStruct((devices, per, LANES), BF16),
        ],
        in_specs=[SMEM, SMEM] + [ANY] * 6,
        out_specs=[ANY, ANY, VMEM, VMEM],
        scratch_shapes=[
            pltpu.VMEM((blocks * MAXK, KEY_SEG, width), BF16),
            pltpu.VMEM((keys, width), BF16),
            pltpu.VMEM((keys, width), BF16),
            pltpu.VMEM((2, SPAN, BOTH), F32),
            pltpu.VMEM((2, SPAN, BOTH), BF16),
            pltpu.VMEM((width, tokens), BF16),
            pltpu.VMEM((SPAN, LANES), BF16),
            pltpu.VMEM((tokens, width), BF16),
            pltpu.VMEM((width, tokens), BF16),
            pltpu.VMEM((width, width), BF16),
            pltpu.VMEM((width, width), BF16),
            pltpu.VMEM((tokens, width), BF16),
            pltpu.SemaphoreType.DMA((blocks,)),
            pltpu.SemaphoreType.DMA((2,)),
            pltpu.SemaphoreType.DMA((5,)),
        ],
        compiler_params=pltpu.CompilerParams(vmem_limit_bytes=60 * MIB),
        cost_estimate=pl.CostEstimate(
            flops=10_000_000_000, bytes_accessed=8 * MIB, transcendentals=4 * MIB),
        name="forward",
    )(sources, counts, fetched, queries, grad_out_t, w_key, w_value, grads)


def backward(sources, counts, keys, values, queries, grad_out, stats, w_key, w_value, devices):
    tokens, width = queries.shape
    blocks = tokens // QUERY_BLOCK
    lines = KEY_SEG * width // LANES
    extra = width * width // (devices * LANES)
    return pl.pallas_call(
        backward_kernel,
        out_shape=[
            jax.ShapeDtypeStruct((devices, lines + extra, LANES), BF16),
            jax.ShapeDtypeStruct((width, tokens), BF16),
        ],
        in_specs=[SMEM, SMEM] + [ANY] * 4 + [VMEM] + [ANY] * 2,
        out_specs=[ANY, VMEM],
        scratch_shapes=[
            pltpu.VMEM((blocks * SPAN, width), BF16),
            pltpu.VMEM((blocks * SPAN, width), BF16),
            pltpu.VMEM((2, SPAN, BOTH), BF16),
            pltpu.VMEM((SPAN, width), BF16),
            pltpu.VMEM((SPAN, width), BF16),
            pltpu.VMEM((devices, KEY_SEG, width), F32),
            pltpu.VMEM((SPAN, LANES), BF16),
            pltpu.VMEM((tokens, width), BF16),
            pltpu.VMEM((tokens, width), BF16),
            pltpu.VMEM((width, width), BF16),
            pltpu.VMEM((width, width), BF16),
            pltpu.VMEM((devices, lines, LANES), BF16),
            pltpu.SemaphoreType.DMA((blocks, 2)),
            pltpu.SemaphoreType.DMA((4,)),
            pltpu.SemaphoreType.DMA,
        ],
        compiler_params=pltpu.CompilerParams(vmem_limit_bytes=60 * MIB),
        cost_estimate=pl.CostEstimate(
            flops=20_000_000_000, bytes_accessed=16 * MIB, transcendentals=4 * MIB),
        name="backward",
    )(sources, counts, keys, values, queries, grad_out, stats, w_key, w_value)


def gather_kernel(wanted, x_ref, out_ref, sem):
    def step(i, carry):
        pltpu.make_async_copy(x_ref.at[jnp.maximum(wanted[i], 0)], out_ref.at[i], sem).start()
        return carry

    lax.fori_loop(0, out_ref.shape[0], step, 0, unroll=8)
    pltpu.make_async_copy(out_ref, out_ref, sem).wait()


def finish_kernel(parts_ref, ret_in, ret_out, wide, sem):
    total = jnp.sum(parts_ref[...].astype(F32), axis=0)
    wide[...] = jnp.broadcast_to(total.astype(BF16)[None], wide.shape)
    extra = wide.shape[1]
    rows = pl.ds(ret_out.shape[1] - extra, extra)
    copy = pltpu.make_async_copy(wide, ret_out.at[:, rows], sem)
    copy.start()
    copy.wait()


def combine_kernel(wanted, back_hbm, base_ref, out_ref, grad_ref, back, acc, sems):
    devices, lines, _ = back.shape
    groups = sems.shape[0]
    size = devices // groups
    width = base_ref.shape[-1]
    slots = width // LANES
    extra = lines - KEY_SEG * slots

    def copy(t):
        part = pl.ds(t * size, size)
        return pltpu.make_async_copy(back_hbm.at[part], back.at[part], sems.at[t])

    for t in range(groups):
        copy(t).start()
    acc[...] = base_ref[...]
    for t in range(groups):
        copy(t).wait()

        def step(i, carry):
            seg = wanted[i]

            @pl.when(seg >= 0)
            def _():
                for u in range(slots):
                    cols = pl.ds(u * LANES, LANES)
                    acc[seg, :, cols] += back[i, pl.ds(u * KEY_SEG, KEY_SEG), :].astype(F32)

            return carry

        lax.fori_loop(t * size, (t + 1) * size, step, 0)
        for i in range(t * size, (t + 1) * size):
            rows = pl.ds((i // slots) * extra, extra)
            cols = pl.ds((i % slots) * LANES, LANES)
            grad_ref[rows, cols] = back[i, pl.ds(lines - extra, extra), :].astype(F32)
    out_ref[...] = acc[...].astype(out_ref.dtype)


def exchange(v):
    return lax.all_to_all(v, AXES, split_axis=0, concat_axis=0, tiled=True)


def local(views_x, dy, w_query, w_key, w_value, w_out, key_lists, key_counts):
    width = views_x.shape[-1]
    x = views_x.reshape(-1, width)
    grads = dy.reshape(-1, width)
    tokens = x.shape[0]
    devices = lax.axis_size(AXES)
    me = lax.axis_index(AXES)
    seg_dev = tokens // KEY_SEG
    blocks = tokens // QUERY_BLOCK
    columns = jnp.arange(MAXK, dtype=jnp.int32)
    live = columns[None, :] < key_counts[:, None]
    asked = live & (key_lists // seg_dev == me)
    wanted = jnp.max(
        jnp.where(asked, key_lists % seg_dev, -1).reshape(devices, blocks * MAXK), axis=1
    )
    outgoing = pl.pallas_call(
        gather_kernel,
        out_shape=jax.ShapeDtypeStruct((devices, KEY_SEG, width), BF16),
        in_specs=[SMEM, ANY],
        out_specs=ANY,
        scratch_shapes=[pltpu.SemaphoreType.DMA],
        name="gather",
    )(wanted, x.reshape(seg_dev, KEY_SEG, width))
    fetched = exchange(outgoing)

    queries = dot(x, w_query).astype(BF16) * BF16(HEAD_DIM ** -0.5)
    grad_out = dot(grads, w_out, 1, 1).astype(BF16)
    grad_out_t = grad_out.T
    sources = lax.dynamic_slice_in_dim(key_lists, me * blocks, blocks, 0).reshape(-1) // seg_dev
    counts = lax.dynamic_slice_in_dim(key_counts, me * blocks, blocks, 0)
    keys, values, stats, pieces = forward(
        sources, counts, fetched, queries, grad_out_t, w_key, w_value, grads
    )
    parts = exchange(pieces)
    ret, dq_t = backward(
        sources, counts, keys, values, queries, grad_out, stats, w_key, w_value, devices
    )
    ret = pl.pallas_call(
        finish_kernel,
        out_shape=jax.ShapeDtypeStruct(ret.shape, ret.dtype),
        in_specs=[VMEM, ANY],
        out_specs=ANY,
        scratch_shapes=[pltpu.VMEM(parts.shape, BF16), pltpu.SemaphoreType.DMA],
        input_output_aliases={1: 0},
        name="finish",
    )(parts, ret)
    back = exchange(ret)
    base = dot(dq_t, w_query, 0, 1)
    grad_x, grad_w_out = pl.pallas_call(
        combine_kernel,
        out_shape=[
            jax.ShapeDtypeStruct((seg_dev, KEY_SEG, width), BF16),
            jax.ShapeDtypeStruct((width, width), F32),
        ],
        in_specs=[SMEM, ANY, VMEM],
        out_specs=[VMEM, VMEM],
        scratch_shapes=[
            pltpu.VMEM(ret.shape, BF16),
            pltpu.VMEM((seg_dev, KEY_SEG, width), F32),
            pltpu.SemaphoreType.DMA((8,)),
        ],
        compiler_params=pltpu.CompilerParams(vmem_limit_bytes=24 * MIB),
        name="combine",
    )(wanted, back, base.reshape(seg_dev, KEY_SEG, width))
    return grad_x.reshape(views_x.shape), grad_w_out


def solution(mesh):
    in_specs = (P("view", "row", None), P("view", "row", None), P(), P(), P(), P(), P(), P())
    out_specs = (P("view", "row", None), P())
    return jax.shard_map(local, mesh=mesh, in_specs=in_specs, out_specs=out_specs, check_vma=False)
```

```python
import jax
import jax.numpy as jnp
from jax import lax
from jax.experimental import pallas as pl
from jax.experimental.pallas import tpu as pltpu
from jax.sharding import PartitionSpec as P

HEAD_DIM = 64
QUERY_BLOCK = 128
KEY_SEG = 32
MAXK = 32
AXES = ("view", "row")
SPAN = MAXK * KEY_SEG
PAIR = 2 * HEAD_DIM
BOTH = 2 * QUERY_BLOCK
LANES = 128
MIB = 1024 * 1024
F32 = jnp.float32
BF16 = jnp.bfloat16
FWD_ROWS = 256
BWD_ROWS = 256
PROJ_ROWS = 256
PROJ_COLS = 256

def dot(a, b, ca=1, cb=0):
    return lax.dot_general(a, b, (((ca,), (cb,)), ((), ())), preferred_element_type=F32)

def split_heads(rows):
    low_half = lax.broadcasted_iota(jnp.int32, rows.shape, 1) < HEAD_DIM
    zero = jnp.zeros_like(rows)
    return jnp.concatenate(
        [jnp.where(low_half, rows, zero), jnp.where(low_half, zero, rows)], axis=0)

def split_channels(cols):
    zero = jnp.zeros((HEAD_DIM, QUERY_BLOCK), cols.dtype)
    return jnp.concatenate(
        [
            jnp.concatenate([cols[:HEAD_DIM], zero], axis=1),
            jnp.concatenate([zero, cols[HEAD_DIM:]], axis=1),
        ],
        axis=0,
    )


def fold(rows, op):
    return op(rows.reshape(rows.shape[0] // 8, 8, rows.shape[-1]), axis=0)

def masked_scores(k_rows, qb, live_rows, start):
    s = dot(k_rows, qb)
    ids = lax.broadcasted_iota(jnp.int32, s.shape, 0)
    return jnp.where(ids < live_rows - start, s, F32(-1e30))

def forward_kernel(
    sources, counts, x_hbm, qt_hbm, gt_hbm, wk_hbm, wv_hbm, dy_hbm,
    k_out, v_out, stat_ref, grad_ref,
    xg, ks, vs, ss, ps, att, qt_ref, gt_ref, wk_ref, wv_ref, dy_ref, sems, osems, wsems,
):
    blocks = qt_ref.shape[1] // QUERY_BLOCK
    width = x_hbm.shape[-1]
    pairs = width // PAIR

    def fetch(b):
        def one(j, carry):
            pltpu.make_async_copy(
                x_hbm.at[sources[b * MAXK + j]], xg.at[b * MAXK + j], sems.at[b]
            ).start()
            return carry
        lax.fori_loop(0, MAXK, one, 0, unroll=8)

    weights = [(wk_hbm, wk_ref), (wv_hbm, wv_ref), (qt_hbm, qt_ref), (gt_hbm, gt_ref), (dy_hbm, dy_ref)]
    loads = [pltpu.make_async_copy(a, z, wsems.at[i]) for i, (a, z) in enumerate(weights)]
    loads[0].start()
    loads[1].start()
    fetch(0)
    for load in loads[2:]:
        load.start()
    loads[0].wait()
    loads[1].wait()

    ncol = 2 * width // PROJ_COLS

    def project(b, c):
        if c == 0:
            mine = xg.at[pl.ds(b * MAXK, MAXK)]
            pltpu.make_async_copy(mine, mine, sems.at[b]).wait()
        half = ncol // 2
        w_ref, dst, hbm, sem = (
            (wk_ref, ks, k_out, osems.at[0]) if c < half else (wv_ref, vs, v_out, osems.at[1])
        )
        cols = pl.ds((c % half) * PROJ_COLS, PROJ_COLS)
        span = pl.ds(b * SPAN, SPAN)
        segs = PROJ_ROWS // KEY_SEG
        for r in range(SPAN // PROJ_ROWS):
            part = xg[pl.ds(b * MAXK + r * segs, segs)].reshape(PROJ_ROWS, width)
            dst[pl.ds(b * SPAN + r * PROJ_ROWS, PROJ_ROWS), cols] = dot(part, w_ref[:, cols]).astype(BF16)
        if c % half == half - 1:
            pltpu.make_async_copy(dst.at[span], hbm.at[span], sem).start()

    state = {}

    def scores(b, p):
        cols = pl.ds(p * PAIR, PAIR)
        tok = pl.ds(b * QUERY_BLOCK, QUERY_BLOCK)
        live_rows = counts[b] * KEY_SEG
        slot = (b * pairs + p) % 2
        qb = split_channels(qt_ref[cols, tok])
        state["top", b, p] = jnp.full((8, BOTH), -1e30, F32)

        def chunk(c):
            rows = pl.ds(c * FWD_ROWS, FWD_ROWS)
            s = masked_scores(ks[pl.ds(b * SPAN + c * FWD_ROWS, FWD_ROWS), cols], qb, live_rows, c * FWD_ROWS)
            ss[slot, rows, :] = s
            state["top", b, p] = jnp.maximum(state["top", b, p], fold(s, jnp.max))

        return [lambda c=c: chunk(c) for c in range(SPAN // FWD_ROWS)]

    def attend(b, p):
        slot = (b * pairs + p) % 2
        top = jnp.max(state["top", b, p], axis=0, keepdims=True)
        state["top", b, p] = top
        state["sum", b, p] = jnp.zeros((8, BOTH), F32)

        def chunk(c):
            rows = pl.ds(c * FWD_ROWS, FWD_ROWS)
            e = jnp.exp(ss[slot, rows, :] - top)
            ps[slot, rows, :] = e.astype(BF16)
            state["sum", b, p] = state["sum", b, p] + fold(e, jnp.sum)

        return [lambda c=c: chunk(c) for c in range(SPAN // FWD_ROWS)]

    def collect(b, p):
        cols = pl.ds(p * PAIR, PAIR)
        tok = pl.ds(b * QUERY_BLOCK, QUERY_BLOCK)
        slot = (b * pairs + p) % 2
        total = jnp.sum(state["sum", b, p], axis=0, keepdims=True)
        inverse = 1.0 / total
        out = dot(vs[pl.ds(b * SPAN, SPAN), cols], ps[slot], 0, 0)
        deltas = []
        for h in range(2):
            here = out[h * HEAD_DIM:(h + 1) * HEAD_DIM, h * QUERY_BLOCK:(h + 1) * QUERY_BLOCK]
            here = here * inverse[:, h * QUERY_BLOCK:(h + 1) * QUERY_BLOCK]
            here = here.astype(BF16)
            chan = pl.ds(p * PAIR + h * HEAD_DIM, HEAD_DIM)
            att[chan, tok] = here
            both = here.astype(F32) * gt_ref[chan, tok].astype(F32)
            deltas.append(jnp.sum(both, axis=0, keepdims=True))
        stat_ref[b, pl.ds(p, 1), :] = state["top", b, p] + jnp.log(total)
        stat_ref[b, pl.ds(pairs + p, 1), :] = jnp.concatenate(deltas, axis=1)

    for b in range(1, blocks):
        fetch(b)
    for c in range(ncol):
        project(0, c)
    for load in loads[2:]:
        load.wait()
    steps = [(b, p) for b in range(blocks) for p in range(pairs)]
    each = ncol // pairs
    for part in scores(*steps[0]):
        part()
    for i, (b, p) in enumerate(steps):
        more = []
        if i + 1 < len(steps):
            if p + 1 == pairs:
                for c in range((pairs - 1) * each, ncol):
                    project(b + 1, c)
            more = scores(*steps[i + 1])
        now = attend(b, p)
        for c in range(len(now)):
            if more and c < len(more):
                more[c]()
            now[c]()
        if b + 1 < blocks and p + 1 < pairs:
            for c in range(p * each, (p + 1) * each):
                project(b + 1, c)
        collect(b, p)
    per = grad_ref.shape[1]
    slots = width // LANES
    for r in range(width // 128):
        g = dot(att[pl.ds(r * 128, 128), :], dy_ref[...]).astype(BF16)
        for i in range(128 // per):
            for t in range(slots):
                grad_ref[(r * (128 // per) + i) * slots + t] = g[
                    i * per:(i + 1) * per, t * LANES:(t + 1) * LANES
                ]
    pltpu.make_async_copy(ks, k_out, osems.at[0]).wait()
    pltpu.make_async_copy(vs, v_out, osems.at[1]).wait()


def backward_kernel(
    sources, counts, first, last, k_hbm, v_hbm, q_hbm, g_hbm, qt_hbm, gt_hbm, stat_ref, wk_hbm, wv_hbm,
    ret_hbm, dq_ref,
    ks, vs, ps, ds, dk, dv, acc, q_ref, g_ref, qt_ref, gt_ref, wk_ref, wv_ref, out, sems, wsems, osem,
):
    blocks = q_ref.shape[0] // QUERY_BLOCK
    width = wk_ref.shape[-1]
    pairs = width // PAIR
    devices = acc.shape[0]
    weights = [
        (qt_hbm, qt_ref), (gt_hbm, gt_ref), (q_hbm, q_ref), (g_hbm, g_ref),
        (wk_hbm, wk_ref), (wv_hbm, wv_ref),
    ]
    loads = [pltpu.make_async_copy(a, z, wsems.at[i]) for i, (a, z) in enumerate(weights)]

    def fetch(b):
        span = pl.ds(b * SPAN, SPAN)
        pltpu.make_async_copy(k_hbm.at[span], ks.at[span], sems.at[b, 0]).start()
        pltpu.make_async_copy(v_hbm.at[span], vs.at[span], sems.at[b, 1]).start()

    loads[0].start()
    loads[1].start()
    fetch(0)
    for load in loads[2:]:
        load.start()
    for b in range(1, blocks):
        fetch(b)
    loads[0].wait()
    loads[1].wait()

    def soft(b, p):
        if p == 0:
            span = pl.ds(b * SPAN, SPAN)
            pltpu.make_async_copy(ks.at[span], ks.at[span], sems.at[b, 0]).wait()
            pltpu.make_async_copy(vs.at[span], vs.at[span], sems.at[b, 1]).wait()
        tok = pl.ds(b * QUERY_BLOCK, QUERY_BLOCK)
        live_rows = counts[b] * KEY_SEG
        slot = (b * pairs + p) % 2
        cols = pl.ds(p * PAIR, PAIR)
        qb = split_channels(qt_ref[cols, tok])
        gb = split_channels(gt_ref[cols, tok])
        lse = stat_ref[b, pl.ds(p, 1), :]
        delta = stat_ref[b, pl.ds(pairs + p, 1), :]

        def chunk(c):
            rows = pl.ds(c * BWD_ROWS, BWD_ROWS)
            there = pl.ds(b * SPAN + c * BWD_ROWS, BWD_ROWS)
            s = masked_scores(ks[there, cols], qb, live_rows, c * BWD_ROWS)
            dp = dot(vs[there, cols], gb)
            w = jnp.exp(s - lse)
            ps[slot, rows, :] = w.astype(BF16)
            ds[slot, rows, :] = (w * (dp - delta)).astype(BF16)

        return [lambda c=c: chunk(c) for c in range(SPAN // BWD_ROWS)]

    def grads(b, p):
        tok = pl.ds(b * QUERY_BLOCK, QUERY_BLOCK)
        slot = (b * pairs + p) % 2
        cols = pl.ds(p * PAIR, PAIR)
        qb = split_heads(q_ref[tok, cols])
        gb = split_heads(g_ref[tok, cols])

        def do_dv():
            dv[b % 2, :, cols] = dot(ps[slot], gb).astype(BF16)

        def do_dk():
            dk[b % 2, :, cols] = dot(ds[slot], qb).astype(BF16)

        def do_dq():
            dq = dot(ks[pl.ds(b * SPAN, SPAN), cols], ds[slot], 0, 0) * F32(HEAD_DIM ** -0.5)
            for h in range(2):
                here = dq[h * HEAD_DIM:(h + 1) * HEAD_DIM, h * QUERY_BLOCK:(h + 1) * QUERY_BLOCK]
                dq_ref[pl.ds(p * PAIR + h * HEAD_DIM, HEAD_DIM), tok] = here.astype(BF16)

        return [do_dv, do_dk, do_dq]

    lines = KEY_SEG * width // LANES
    per = SPAN // pairs
    segs = per // KEY_SEG

    def back(b, c):
        rows = pl.ds(c * per, per)
        term = dot(dk[b % 2, rows, :], wk_ref[...]) + dot(dv[b % 2, rows, :], wv_ref[...])
        for j in range(segs):
            entry = b * MAXK + c * segs + j
            slot = sources[entry]
            mine = term[j * KEY_SEG:(j + 1) * KEY_SEG, :]
            if b:
                mine = jnp.where(first[entry] > 0, mine, acc[slot] + mine)
            if b + 1 < blocks:
                acc[slot] = mine
            low = mine.astype(BF16)
            for u in range(width // LANES):
                out[slot, pl.ds(u * KEY_SEG, KEY_SEG), :] = low[:, u * LANES:(u + 1) * LANES]

    def line(entry):
        slot = sources[entry]
        return pltpu.make_async_copy(out.at[slot], ret_hbm.at[slot, pl.ds(0, lines)], osem)

    def send(start, size):
        def one(entry, carry):
            @pl.when(last[entry] > 0)
            def _():
                line(entry).start()

            return carry

        lax.fori_loop(start, start + size, one, 0, unroll=4)

    steps = [(b, p) for b in range(blocks) for p in range(pairs)]
    for i in range(len(steps) + 1):
        now = soft(*steps[i]) if i < len(steps) else []
        if i == 1:
            loads[2].wait()
            loads[3].wait()
        old = grads(*steps[i - 1]) if i else []
        for c in range(max(len(now), len(old))):
            if c < len(now):
                now[c]()
            if c < len(old):
                old[c]()
        if i == 1:
            for load in loads[4:]:
                load.wait()
        if i and steps[i - 1][0]:
            back(steps[i - 1][0] - 1, steps[i - 1][1])
            if steps[i - 1][1] == pairs - 1:
                send((steps[i - 1][0] - 1) * MAXK, MAXK)
    for p in range(pairs):
        back(blocks - 1, p)
        send((blocks - 1) * MAXK + p * segs, segs)

    def finish(entry, carry):
        @pl.when(last[entry] > 0)
        def _():
            line(entry).wait()

        return carry

    lax.fori_loop(0, blocks * MAXK, finish, 0, unroll=4)


VMEM = pl.BlockSpec(memory_space=pltpu.VMEM)
SMEM = pl.BlockSpec(memory_space=pltpu.SMEM)
ANY = pl.BlockSpec(memory_space=pl.ANY)

def square(width, tokens):
    return pltpu.VMEM((tokens, width), BF16)

def forward(sources, counts, fetched, queries_t, grad_out_t, w_key, w_value, grads):
    devices, _, width = fetched.shape
    tokens = queries_t.shape[1]
    blocks = tokens // QUERY_BLOCK
    keys = blocks * SPAN
    per = width * width // (devices * LANES)
    return pl.pallas_call(
        forward_kernel,
        out_shape=[
            jax.ShapeDtypeStruct((keys, width), BF16),
            jax.ShapeDtypeStruct((keys, width), BF16),
            jax.ShapeDtypeStruct((blocks, 2 * width // PAIR, BOTH), F32),
            jax.ShapeDtypeStruct((devices, per, LANES), BF16),
        ],
        in_specs=[SMEM, SMEM] + [ANY] * 6,
        out_specs=[ANY, ANY, VMEM, VMEM],
        scratch_shapes=[
            pltpu.VMEM((blocks * MAXK, KEY_SEG, width), BF16),
            pltpu.VMEM((keys, width), BF16),
            pltpu.VMEM((keys, width), BF16),
            pltpu.VMEM((2, SPAN, BOTH), F32),
            pltpu.VMEM((2, SPAN, BOTH), BF16),
            pltpu.VMEM((width, tokens), BF16),
            pltpu.VMEM((tokens, width), BF16),
            pltpu.VMEM((width, tokens), BF16),
            pltpu.VMEM((width, width), BF16),
            pltpu.VMEM((width, width), BF16),
            pltpu.VMEM((tokens, width), BF16),
            pltpu.SemaphoreType.DMA((blocks,)),
            pltpu.SemaphoreType.DMA((2,)),
            pltpu.SemaphoreType.DMA((5,)),
        ],
        compiler_params=pltpu.CompilerParams(vmem_limit_bytes=60 * MIB),
        cost_estimate=pl.CostEstimate(
            flops=10_000_000_000, bytes_accessed=8 * MIB, transcendentals=4 * MIB),
        name="forward",
    )(sources, counts, fetched, queries_t, grad_out_t, w_key, w_value, grads)


def backward(sources, counts, first, last, keys, values, queries, grad_out, queries_t, grad_out_t, stats, w_key, w_value, devices):
    tokens, width = queries.shape
    blocks = tokens // QUERY_BLOCK
    lines = KEY_SEG * width // LANES
    extra = width * width // (devices * LANES)
    return pl.pallas_call(
        backward_kernel,
        out_shape=[
            jax.ShapeDtypeStruct((devices, lines + extra, LANES), BF16),
            jax.ShapeDtypeStruct((width, tokens), BF16),
        ],
        in_specs=[SMEM] * 4 + [ANY] * 6 + [VMEM] + [ANY] * 2,
        out_specs=[ANY, VMEM],
        scratch_shapes=[
            pltpu.VMEM((blocks * SPAN, width), BF16),
            pltpu.VMEM((blocks * SPAN, width), BF16),
            pltpu.VMEM((2, SPAN, BOTH), BF16),
            pltpu.VMEM((2, SPAN, BOTH), BF16),
            pltpu.VMEM((2, SPAN, width), BF16),
            pltpu.VMEM((2, SPAN, width), BF16),
            pltpu.VMEM((devices, KEY_SEG, width), F32),
            pltpu.VMEM((tokens, width), BF16),
            pltpu.VMEM((tokens, width), BF16),
            pltpu.VMEM((width, tokens), BF16),
            pltpu.VMEM((width, tokens), BF16),
            pltpu.VMEM((width, width), BF16),
            pltpu.VMEM((width, width), BF16),
            pltpu.VMEM((devices, lines, LANES), BF16),
            pltpu.SemaphoreType.DMA((blocks, 2)),
            pltpu.SemaphoreType.DMA((6,)),
            pltpu.SemaphoreType.DMA,
        ],
        compiler_params=pltpu.CompilerParams(vmem_limit_bytes=60 * MIB),
        cost_estimate=pl.CostEstimate(
            flops=20_000_000_000, bytes_accessed=16 * MIB, transcendentals=4 * MIB),
        name="backward",
              )(sources, counts, first, last, keys, values, queries, grad_out, queries_t, grad_out_t, stats, w_key, w_value)


def gather_kernel(wanted, x_hbm, out_ref, x_ref, sems):
    load = pltpu.make_async_copy(x_hbm, x_ref, sems.at[0])
    load.start()
    load.wait()

    def step(i, carry):
        pltpu.make_async_copy(
            x_ref.at[jnp.maximum(wanted[i], 0)], out_ref.at[i], sems.at[1]
        ).start()
        return carry

    lax.fori_loop(0, out_ref.shape[0], step, 0, unroll=8)
    pltpu.make_async_copy(out_ref, out_ref, sems.at[1]).wait()


def finish_kernel(parts_ref, ret_in, ret_out, wide, sem):
    total = jnp.sum(parts_ref[...].astype(F32), axis=0)
    wide[...] = jnp.broadcast_to(total.astype(BF16)[None], wide.shape)
    extra = wide.shape[1]
    rows = pl.ds(ret_out.shape[1] - extra, extra)
    copy = pltpu.make_async_copy(wide, ret_out.at[:, rows], sem)
    copy.start()
    copy.wait()


def combine_kernel(wanted, back_hbm, base_ref, out_ref, grad_ref, back, acc, sems):
    devices, lines, _ = back.shape
    groups = sems.shape[0]
    size = devices // groups
    width = base_ref.shape[-1]
    slots = width // LANES
    extra = lines - KEY_SEG * slots

    def copy(t):
        part = pl.ds(t * size, size)
        return pltpu.make_async_copy(back_hbm.at[part], back.at[part], sems.at[t])

    for t in range(groups):
        copy(t).start()
    acc[...] = base_ref[...]
    for t in range(groups):
        copy(t).wait()

        def step(i, carry):
            seg = wanted[i]

            @pl.when(seg >= 0)
            def _():
                for u in range(slots):
                    cols = pl.ds(u * LANES, LANES)
                    acc[seg, :, cols] += back[i, pl.ds(u * KEY_SEG, KEY_SEG), :].astype(F32)

            return carry

        lax.fori_loop(t * size, (t + 1) * size, step, 0)
        for i in range(t * size, (t + 1) * size):
            rows = pl.ds((i // slots) * extra, extra)
            cols = pl.ds((i % slots) * LANES, LANES)
            grad_ref[rows, cols] = back[i, pl.ds(lines - extra, extra), :].astype(F32)
    out_ref[...] = acc[...].astype(out_ref.dtype)


def exchange(v):
    return lax.all_to_all(v, AXES, split_axis=0, concat_axis=0, tiled=True)


def local(views_x, dy, w_query, w_key, w_value, w_out, key_lists, key_counts):
    width = views_x.shape[-1]
    x = views_x.reshape(-1, width)
    grads = dy.reshape(-1, width)
    tokens = x.shape[0]
    devices = lax.axis_size(AXES)
    me = lax.axis_index(AXES)
    seg_dev = tokens // KEY_SEG
    blocks = tokens // QUERY_BLOCK
    columns = jnp.arange(MAXK, dtype=jnp.int32)
    live = columns[None, :] < key_counts[:, None]
    asked = live & (key_lists // seg_dev == me)
    wanted = jnp.max(
        jnp.where(asked, key_lists % seg_dev, -1).reshape(devices, blocks * MAXK), axis=1
    )
    outgoing = pl.pallas_call(
        gather_kernel,
        out_shape=jax.ShapeDtypeStruct((devices, KEY_SEG, width), BF16),
        in_specs=[SMEM, ANY],
        out_specs=ANY,
        scratch_shapes=[
            pltpu.VMEM((seg_dev, KEY_SEG, width), BF16),
            pltpu.SemaphoreType.DMA((2,)),
        ],
        name="gather",
    )(wanted, x.reshape(seg_dev, KEY_SEG, width))
    fetched = exchange(outgoing)

    queries = dot(x, w_query).astype(BF16) * BF16(HEAD_DIM ** -0.5)
    grad_out = dot(grads, w_out, 1, 1).astype(BF16)
    queries_t = queries.T
    grad_out_t = grad_out.T
    mine = lax.dynamic_slice_in_dim(key_lists, me * blocks, blocks, 0)
    counts = lax.dynamic_slice_in_dim(key_counts, me * blocks, blocks, 0)
    sources = jnp.where(columns[None, :] < counts[:, None], mine // seg_dev, me).reshape(-1)
    entry = jnp.arange(blocks * MAXK, dtype=jnp.int32)
    same = sources[:, None] == sources[None, :]
    first = 1 - jnp.any(same & (entry[None, :] < entry[:, None]), axis=1).astype(jnp.int32)
    last = 1 - jnp.any(same & (entry[None, :] > entry[:, None]), axis=1).astype(jnp.int32)
    keys, values, stats, pieces = forward(
        sources, counts, fetched, queries_t, grad_out_t, w_key, w_value, grads
    )
    parts = exchange(pieces)
    ret, dq_t = backward(
        sources, counts, first, last, keys, values, queries, grad_out, queries_t, grad_out_t,
        stats, w_key.T, w_value.T, devices
    )
    ret = pl.pallas_call(
        finish_kernel,
        out_shape=jax.ShapeDtypeStruct(ret.shape, ret.dtype),
        in_specs=[VMEM, ANY],
        out_specs=ANY,
        scratch_shapes=[pltpu.VMEM(parts.shape, BF16), pltpu.SemaphoreType.DMA],
        input_output_aliases={1: 0},
        name="finish",
    )(parts, ret)
    back = exchange(ret)
    base = dot(dq_t, w_query, 0, 1)
    grad_x, grad_w_out = pl.pallas_call(
        combine_kernel,
        out_shape=[
            jax.ShapeDtypeStruct((seg_dev, KEY_SEG, width), BF16),
            jax.ShapeDtypeStruct((width, width), F32),
        ],
        in_specs=[SMEM, ANY, VMEM],
        out_specs=[VMEM, VMEM],
        scratch_shapes=[
            pltpu.VMEM(ret.shape, BF16),
            pltpu.VMEM((seg_dev, KEY_SEG, width), F32),
            pltpu.SemaphoreType.DMA((8,)),
        ],
        compiler_params=pltpu.CompilerParams(vmem_limit_bytes=24 * MIB),
        name="combine",
    )(wanted, back, base.reshape(seg_dev, KEY_SEG, width))
    return grad_x.reshape(views_x.shape), grad_w_out


def solution(mesh):
    in_specs = (P("view", "row", None), P("view", "row", None), P(), P(), P(), P(), P(), P())
    out_specs = (P("view", "row", None), P())
    return jax.shard_map(local, mesh=mesh, in_specs=in_specs, out_specs=out_specs, check_vma=False)
```

```python
import jax
import jax.numpy as jnp
from jax import lax
from jax.experimental import pallas as pl
from jax.experimental.pallas import tpu as pltpu
from jax.sharding import PartitionSpec as P

HEAD_DIM = 64
QUERY_BLOCK = 128
KEY_SEG = 32
MAXK = 32
AXES = ("view", "row")
SPAN = MAXK * KEY_SEG
PAIR = 2 * HEAD_DIM
BOTH = 2 * QUERY_BLOCK
LANES = 128
MIB = 1024 * 1024
F32 = jnp.float32
BF16 = jnp.bfloat16
FWD_ROWS = 256
BWD_ROWS = 256
PROJ_ROWS = 256
PROJ_COLS = 256

def dot(a, b, ca=1, cb=0):
    return lax.dot_general(a, b, (((ca,), (cb,)), ((), ())), preferred_element_type=F32)

def split_heads(rows):
    low_half = lax.broadcasted_iota(jnp.int32, rows.shape, 1) < HEAD_DIM
    zero = jnp.zeros_like(rows)
    return jnp.concatenate(
        [jnp.where(low_half, rows, zero), jnp.where(low_half, zero, rows)], axis=0)

def split_channels(cols):
    zero = jnp.zeros((HEAD_DIM, QUERY_BLOCK), cols.dtype)
    return jnp.concatenate(
        [
            jnp.concatenate([cols[:HEAD_DIM], zero], axis=1),
            jnp.concatenate([zero, cols[HEAD_DIM:]], axis=1),
        ],
        axis=0,
    )


def fold(rows, op):
    return op(rows.reshape(rows.shape[0] // 8, 8, rows.shape[-1]), axis=0)

def masked_scores(k_rows, qb, live_rows, start):
    s = dot(k_rows, qb)
    ids = lax.broadcasted_iota(jnp.int32, s.shape, 0)
    return jnp.where(ids < live_rows - start, s, F32(-1e30))

def forward_kernel(
    sources, counts, x_hbm, qt_hbm, gt_hbm, wk_hbm, wv_hbm, dy_hbm,
    k_out, v_out, stat_ref, grad_ref,
    xg, ks, vs, ss, ps, att, qt_ref, gt_ref, wk_ref, wv_ref, dy_ref, sems, osems, wsems,
):
    blocks = qt_ref.shape[1] // QUERY_BLOCK
    width = x_hbm.shape[-1]
    pairs = width // PAIR

    def fetch(b):
        def one(j, carry):
            pltpu.make_async_copy(
                x_hbm.at[sources[b * MAXK + j]], xg.at[b * MAXK + j], sems.at[b]
            ).start()
            return carry
        lax.fori_loop(0, MAXK, one, 0, unroll=8)

    weights = [(wk_hbm, wk_ref), (wv_hbm, wv_ref), (qt_hbm, qt_ref), (gt_hbm, gt_ref), (dy_hbm, dy_ref)]
    loads = [pltpu.make_async_copy(a, z, wsems.at[i]) for i, (a, z) in enumerate(weights)]
    loads[0].start()
    loads[1].start()
    fetch(0)
    for load in loads[2:]:
        load.start()
    loads[0].wait()
    loads[1].wait()

    ncol = 2 * width // PROJ_COLS

    def project(b, c):
        if c == 0:
            mine = xg.at[pl.ds(b * MAXK, MAXK)]
            pltpu.make_async_copy(mine, mine, sems.at[b]).wait()
        half = ncol // 2
        w_ref, dst, hbm, sem = (
            (wk_ref, ks, k_out, osems.at[0]) if c < half else (wv_ref, vs, v_out, osems.at[1])
        )
        cols = pl.ds((c % half) * PROJ_COLS, PROJ_COLS)
        span = pl.ds(b * SPAN, SPAN)
        segs = PROJ_ROWS // KEY_SEG
        for r in range(SPAN // PROJ_ROWS):
            part = xg[pl.ds(b * MAXK + r * segs, segs)].reshape(PROJ_ROWS, width)
            dst[pl.ds(b * SPAN + r * PROJ_ROWS, PROJ_ROWS), cols] = dot(part, w_ref[:, cols]).astype(BF16)
        if c % half == half - 1:
            pltpu.make_async_copy(dst.at[span], hbm.at[span], sem).start()

    state = {}

    def scores(b, p):
        cols = pl.ds(p * PAIR, PAIR)
        tok = pl.ds(b * QUERY_BLOCK, QUERY_BLOCK)
        live_rows = counts[b] * KEY_SEG
        slot = (b * pairs + p) % 2
        qb = split_channels(qt_ref[cols, tok])
        state["top", b, p] = jnp.full((8, BOTH), -1e30, F32)

        def chunk(c):
            rows = pl.ds(c * FWD_ROWS, FWD_ROWS)
            s = masked_scores(ks[pl.ds(b * SPAN + c * FWD_ROWS, FWD_ROWS), cols], qb, live_rows, c * FWD_ROWS)
            ss[slot, rows, :] = s
            state["top", b, p] = jnp.maximum(state["top", b, p], fold(s, jnp.max))

        return [lambda c=c: chunk(c) for c in range(SPAN // FWD_ROWS)]

    def attend(b, p):
        slot = (b * pairs + p) % 2
        top = jnp.max(state["top", b, p], axis=0, keepdims=True)
        state["top", b, p] = top
        state["sum", b, p] = jnp.zeros((8, BOTH), F32)

        def chunk(c):
            rows = pl.ds(c * FWD_ROWS, FWD_ROWS)
            e = jnp.exp(ss[slot, rows, :] - top)
            ps[slot, rows, :] = e.astype(BF16)
            state["sum", b, p] = state["sum", b, p] + fold(e, jnp.sum)

        return [lambda c=c: chunk(c) for c in range(SPAN // FWD_ROWS)]

    def collect(b, p):
        cols = pl.ds(p * PAIR, PAIR)
        tok = pl.ds(b * QUERY_BLOCK, QUERY_BLOCK)
        slot = (b * pairs + p) % 2
        total = jnp.sum(state["sum", b, p], axis=0, keepdims=True)
        inverse = 1.0 / total
        out = dot(vs[pl.ds(b * SPAN, SPAN), cols], ps[slot], 0, 0)
        deltas = []
        for h in range(2):
            here = out[h * HEAD_DIM:(h + 1) * HEAD_DIM, h * QUERY_BLOCK:(h + 1) * QUERY_BLOCK]
            here = here * inverse[:, h * QUERY_BLOCK:(h + 1) * QUERY_BLOCK]
            here = here.astype(BF16)
            chan = pl.ds(p * PAIR + h * HEAD_DIM, HEAD_DIM)
            att[chan, tok] = here
            both = here.astype(F32) * gt_ref[chan, tok].astype(F32)
            deltas.append(jnp.sum(both, axis=0, keepdims=True))
        stat_ref[b, pl.ds(p, 1), :] = state["top", b, p] + jnp.log(total)
        stat_ref[b, pl.ds(pairs + p, 1), :] = jnp.concatenate(deltas, axis=1)

    for b in range(1, blocks):
        fetch(b)
    for c in range(ncol):
        project(0, c)
    for load in loads[2:]:
        load.wait()
    steps = [(b, p) for b in range(blocks) for p in range(pairs)]
    each = ncol // pairs
    for part in scores(*steps[0]):
        part()
    for i, (b, p) in enumerate(steps):
        more = []
        if i + 1 < len(steps):
            if p + 1 == pairs:
                for c in range((pairs - 1) * each, ncol):
                    project(b + 1, c)
            more = scores(*steps[i + 1])
        now = attend(b, p)
        for c in range(len(now)):
            if more and c < len(more):
                more[c]()
            now[c]()
        if b + 1 < blocks and p + 1 < pairs:
            for c in range(p * each, (p + 1) * each):
                project(b + 1, c)
        collect(b, p)
    per = grad_ref.shape[1]
    slots = width // LANES
    for r in range(width // 128):
        g = dot(att[pl.ds(r * 128, 128), :], dy_ref[...]).astype(BF16)
        for i in range(128 // per):
            for t in range(slots):
                grad_ref[(r * (128 // per) + i) * slots + t] = g[
                    i * per:(i + 1) * per, t * LANES:(t + 1) * LANES
                ]
    pltpu.make_async_copy(ks, k_out, osems.at[0]).wait()
    pltpu.make_async_copy(vs, v_out, osems.at[1]).wait()


def backward_kernel(
    sources, counts, first, last, k_hbm, v_hbm, q_hbm, g_hbm, qt_hbm, gt_hbm, stat_ref, wk_hbm, wv_hbm,
    ret_hbm, dq_ref,
    ks, vs, ps, ds, dk, dv, acc, q_ref, g_ref, qt_ref, gt_ref, wk_ref, wv_ref, out, sems, wsems, osem,
):
    blocks = q_ref.shape[0] // QUERY_BLOCK
    width = wk_ref.shape[-1]
    pairs = width // PAIR
    devices = acc.shape[0]
    weights = [
        (qt_hbm, qt_ref), (gt_hbm, gt_ref), (q_hbm, q_ref), (g_hbm, g_ref),
        (wk_hbm, wk_ref), (wv_hbm, wv_ref),
    ]
    loads = [pltpu.make_async_copy(a, z, wsems.at[i]) for i, (a, z) in enumerate(weights)]

    def fetch(b):
        span = pl.ds(b * SPAN, SPAN)
        pltpu.make_async_copy(k_hbm.at[span], ks.at[span], sems.at[b, 0]).start()
        pltpu.make_async_copy(v_hbm.at[span], vs.at[span], sems.at[b, 1]).start()

    loads[0].start()
    loads[1].start()
    fetch(0)
    for load in loads[2:]:
        load.start()
    for b in range(1, blocks):
        fetch(b)
    loads[0].wait()
    loads[1].wait()

    def soft(b, p):
        if p == 0:
            span = pl.ds(b * SPAN, SPAN)
            pltpu.make_async_copy(ks.at[span], ks.at[span], sems.at[b, 0]).wait()
            pltpu.make_async_copy(vs.at[span], vs.at[span], sems.at[b, 1]).wait()
        tok = pl.ds(b * QUERY_BLOCK, QUERY_BLOCK)
        live_rows = counts[b] * KEY_SEG
        slot = (b * pairs + p) % 2
        cols = pl.ds(p * PAIR, PAIR)
        qb = split_channels(qt_ref[cols, tok])
        gb = split_channels(gt_ref[cols, tok])
        lse = stat_ref[b, pl.ds(p, 1), :]
        delta = stat_ref[b, pl.ds(pairs + p, 1), :]

        def chunk(c):
            rows = pl.ds(c * BWD_ROWS, BWD_ROWS)
            there = pl.ds(b * SPAN + c * BWD_ROWS, BWD_ROWS)
            s = masked_scores(ks[there, cols], qb, live_rows, c * BWD_ROWS)
            dp = dot(vs[there, cols], gb)
            w = jnp.exp(s - lse)
            ps[slot, rows, :] = w.astype(BF16)
            ds[slot, rows, :] = (w * (dp - delta)).astype(BF16)

        return [lambda c=c: chunk(c) for c in range(SPAN // BWD_ROWS)]

    def grads(b, p):
        tok = pl.ds(b * QUERY_BLOCK, QUERY_BLOCK)
        slot = (b * pairs + p) % 2
        cols = pl.ds(p * PAIR, PAIR)
        qb = split_heads(q_ref[tok, cols])
        gb = split_heads(g_ref[tok, cols])

        def do_dv():
            dv[b % 2, :, cols] = dot(ps[slot], gb).astype(BF16)

        def do_dk():
            dk[b % 2, :, cols] = dot(ds[slot], qb).astype(BF16)

        def do_dq():
            dq = dot(ks[pl.ds(b * SPAN, SPAN), cols], ds[slot], 0, 0) * F32(HEAD_DIM ** -0.5)
            for h in range(2):
                here = dq[h * HEAD_DIM:(h + 1) * HEAD_DIM, h * QUERY_BLOCK:(h + 1) * QUERY_BLOCK]
                dq_ref[pl.ds(p * PAIR + h * HEAD_DIM, HEAD_DIM), tok] = here.astype(BF16)

        return [do_dv, do_dk, do_dq]

    lines = KEY_SEG * width // LANES
    per = SPAN // pairs
    segs = per // KEY_SEG

    def back(b, c):
        rows = pl.ds(c * per, per)
        term = dot(dk[b % 2, rows, :], wk_ref[...]) + dot(dv[b % 2, rows, :], wv_ref[...])
        for j in range(segs):
            entry = b * MAXK + c * segs + j
            slot = sources[entry]
            mine = term[j * KEY_SEG:(j + 1) * KEY_SEG, :]
            if b:
                mine = jnp.where(first[entry] > 0, mine, acc[slot] + mine)
            if b + 1 < blocks:
                acc[slot] = mine
            low = mine.astype(BF16)
            for u in range(width // LANES):
                out[slot, pl.ds(u * KEY_SEG, KEY_SEG), :] = low[:, u * LANES:(u + 1) * LANES]

    def line(entry):
        slot = sources[entry]
        return pltpu.make_async_copy(out.at[slot], ret_hbm.at[slot, pl.ds(0, lines)], osem)

    def send(start, size):
        def one(entry, carry):
            @pl.when(last[entry] > 0)
            def _():
                line(entry).start()

            return carry

        lax.fori_loop(start, start + size, one, 0, unroll=4)

    steps = [(b, p) for b in range(blocks) for p in range(pairs)]
    for i in range(len(steps) + 1):
        now = soft(*steps[i]) if i < len(steps) else []
        if i == 1:
            loads[2].wait()
            loads[3].wait()
        old = grads(*steps[i - 1]) if i else []
        for c in range(max(len(now), len(old))):
            if c < len(now):
                now[c]()
            if c < len(old):
                old[c]()
        if i == 1:
            for load in loads[4:]:
                load.wait()
        if i and steps[i - 1][0]:
            back(steps[i - 1][0] - 1, steps[i - 1][1])
            if steps[i - 1][1] == pairs - 1:
                send((steps[i - 1][0] - 1) * MAXK, MAXK)
    for p in range(pairs):
        back(blocks - 1, p)
        send((blocks - 1) * MAXK + p * segs, segs)

    def finish(entry, carry):
        @pl.when(last[entry] > 0)
        def _():
            line(entry).wait()

        return carry

    lax.fori_loop(0, blocks * MAXK, finish, 0, unroll=4)


VMEM = pl.BlockSpec(memory_space=pltpu.VMEM)
SMEM = pl.BlockSpec(memory_space=pltpu.SMEM)
ANY = pl.BlockSpec(memory_space=pl.ANY)

def square(width, tokens):
    return pltpu.VMEM((tokens, width), BF16)

def forward(sources, counts, fetched, queries_t, grad_out_t, w_key, w_value, grads):
    devices, _, width = fetched.shape
    tokens = queries_t.shape[1]
    blocks = tokens // QUERY_BLOCK
    keys = blocks * SPAN
    per = width * width // (devices * LANES)
    return pl.pallas_call(
        forward_kernel,
        out_shape=[
            jax.ShapeDtypeStruct((keys, width), BF16),
            jax.ShapeDtypeStruct((keys, width), BF16),
            jax.ShapeDtypeStruct((blocks, 2 * width // PAIR, BOTH), F32),
            jax.ShapeDtypeStruct((devices, per, LANES), BF16),
        ],
        in_specs=[SMEM, SMEM] + [ANY] * 6,
        out_specs=[ANY, ANY, VMEM, VMEM],
        scratch_shapes=[
            pltpu.VMEM((blocks * MAXK, KEY_SEG, width), BF16),
            pltpu.VMEM((keys, width), BF16),
            pltpu.VMEM((keys, width), BF16),
            pltpu.VMEM((2, SPAN, BOTH), F32),
            pltpu.VMEM((2, SPAN, BOTH), BF16),
            pltpu.VMEM((width, tokens), BF16),
            pltpu.VMEM((tokens, width), BF16),
            pltpu.VMEM((width, tokens), BF16),
            pltpu.VMEM((width, width), BF16),
            pltpu.VMEM((width, width), BF16),
            pltpu.VMEM((tokens, width), BF16),
            pltpu.SemaphoreType.DMA((blocks,)),
            pltpu.SemaphoreType.DMA((2,)),
            pltpu.SemaphoreType.DMA((5,)),
        ],
        compiler_params=pltpu.CompilerParams(vmem_limit_bytes=60 * MIB),
        cost_estimate=pl.CostEstimate(
            flops=10_000_000_000, bytes_accessed=8 * MIB, transcendentals=4 * MIB),
        name="forward",
    )(sources, counts, fetched, queries_t, grad_out_t, w_key, w_value, grads)


def backward(sources, counts, first, last, keys, values, queries, grad_out, queries_t, grad_out_t, stats, w_key, w_value, devices):
    tokens, width = queries.shape
    blocks = tokens // QUERY_BLOCK
    lines = KEY_SEG * width // LANES
    extra = width * width // (devices * LANES)
    return pl.pallas_call(
        backward_kernel,
        out_shape=[
            jax.ShapeDtypeStruct((devices, lines + extra, LANES), BF16),
            jax.ShapeDtypeStruct((width, tokens), BF16),
        ],
        in_specs=[SMEM] * 4 + [ANY] * 6 + [VMEM] + [ANY] * 2,
        out_specs=[ANY, VMEM],
        scratch_shapes=[
            pltpu.VMEM((blocks * SPAN, width), BF16),
            pltpu.VMEM((blocks * SPAN, width), BF16),
            pltpu.VMEM((2, SPAN, BOTH), BF16),
            pltpu.VMEM((2, SPAN, BOTH), BF16),
            pltpu.VMEM((2, SPAN, width), BF16),
            pltpu.VMEM((2, SPAN, width), BF16),
            pltpu.VMEM((devices, KEY_SEG, width), F32),
            pltpu.VMEM((tokens, width), BF16),
            pltpu.VMEM((tokens, width), BF16),
            pltpu.VMEM((width, tokens), BF16),
            pltpu.VMEM((width, tokens), BF16),
            pltpu.VMEM((width, width), BF16),
            pltpu.VMEM((width, width), BF16),
            pltpu.VMEM((devices, lines, LANES), BF16),
            pltpu.SemaphoreType.DMA((blocks, 2)),
            pltpu.SemaphoreType.DMA((6,)),
            pltpu.SemaphoreType.DMA,
        ],
        compiler_params=pltpu.CompilerParams(vmem_limit_bytes=60 * MIB),
        cost_estimate=pl.CostEstimate(
            flops=20_000_000_000, bytes_accessed=16 * MIB, transcendentals=4 * MIB),
        name="backward",
              )(sources, counts, first, last, keys, values, queries, grad_out, queries_t, grad_out_t, stats, w_key, w_value)


def gather_kernel(block_max, x_hbm, out_ref, x_ref, sems):
    load = pltpu.make_async_copy(x_hbm, x_ref, sems.at[0])
    load.start()
    load.wait()
    blocks = block_max.shape[0] // out_ref.shape[0]

    def step(i, carry):
        seg = jnp.int32(0)
        for k in range(blocks):
            seg = jnp.maximum(seg, block_max[i * blocks + k])
        pltpu.make_async_copy(x_ref.at[seg], out_ref.at[i], sems.at[1]).start()
        return carry

    lax.fori_loop(0, out_ref.shape[0], step, 0, unroll=8)
    pltpu.make_async_copy(out_ref, out_ref, sems.at[1]).wait()


def finish_kernel(parts_hbm, ret_in, ret_out, parts_ref, wide, sem):
    load = pltpu.make_async_copy(parts_hbm, parts_ref, sem)
    load.start()
    load.wait()
    total = jnp.sum(parts_ref[...].astype(F32), axis=0)
    wide[...] = jnp.broadcast_to(total.astype(BF16)[None], wide.shape)
    extra = wide.shape[1]
    rows = pl.ds(ret_out.shape[1] - extra, extra)
    copy = pltpu.make_async_copy(wide, ret_out.at[:, rows], sem)
    copy.start()
    copy.wait()


def combine_kernel(
    wanted, back_hbm, base_ref, out_hbm, grad_hbm, back, acc, wide, grad, out, sems, ends
):
    devices, extra, _ = wide.shape
    width = base_ref.shape[-1]
    slots = width // LANES
    lines = KEY_SEG * slots
    tail = pltpu.make_async_copy(back_hbm.at[:, pl.ds(lines, extra)], wide, ends.at[0])
    tail.start()

    def line(i):
        return pltpu.make_async_copy(back_hbm.at[i, pl.ds(0, lines)], back.at[i], sems.at[i])

    def fetch(i, carry):
        @pl.when(wanted[i] >= 0)
        def _():
            line(i).start()

        return carry

    lax.fori_loop(0, devices, fetch, 0, unroll=4)
    acc[...] = base_ref[...]
    tail.wait()
    for i in range(devices):
        rows = pl.ds((i // slots) * extra, extra)
        cols = pl.ds((i % slots) * LANES, LANES)
        grad[rows, cols] = wide[i].astype(F32)
    grad_out = pltpu.make_async_copy(grad, grad_hbm, ends.at[1])
    grad_out.start()

    def add(i, carry):
        seg = wanted[i]

        @pl.when(seg >= 0)
        def _():
            line(i).wait()
            for u in range(slots):
                cols = pl.ds(u * LANES, LANES)
                acc[seg, :, cols] += back[i, pl.ds(u * KEY_SEG, KEY_SEG), :].astype(F32)

        return carry

    lax.fori_loop(0, devices, add, 0)
    out[...] = acc[...].astype(out.dtype)
    x_out = pltpu.make_async_copy(out, out_hbm, ends.at[2])
    x_out.start()
    x_out.wait()
    grad_out.wait()


def exchange(v):
    return lax.all_to_all(v, AXES, split_axis=0, concat_axis=0, tiled=True)


def local(views_x, dy, w_query, w_key, w_value, w_out, key_lists, key_counts):
    width = views_x.shape[-1]
    x = views_x.reshape(-1, width)
    grads = dy.reshape(-1, width)
    tokens = x.shape[0]
    devices = lax.axis_size(AXES)
    me = lax.axis_index(AXES)
    seg_dev = tokens // KEY_SEG
    blocks = tokens // QUERY_BLOCK
    columns = jnp.arange(MAXK, dtype=jnp.int32)
    live = columns[None, :] < key_counts[:, None]
    asked = live & (key_lists // seg_dev == me)
    block_max = jnp.max(jnp.where(asked, key_lists % seg_dev, -1), axis=1)
    wanted = jnp.max(block_max.reshape(devices, blocks), axis=1)
    outgoing = pl.pallas_call(
        gather_kernel,
        out_shape=jax.ShapeDtypeStruct((devices, KEY_SEG, width), BF16),
        in_specs=[SMEM, ANY],
        out_specs=ANY,
        scratch_shapes=[
            pltpu.VMEM((seg_dev, KEY_SEG, width), BF16),
            pltpu.SemaphoreType.DMA((2,)),
        ],
        name="gather",
    )(block_max, x.reshape(seg_dev, KEY_SEG, width))
    fetched = exchange(outgoing)

    queries = dot(x, w_query).astype(BF16) * BF16(HEAD_DIM ** -0.5)
    grad_out = dot(grads, w_out, 1, 1).astype(BF16)
    queries_t = queries.T
    grad_out_t = grad_out.T
    mine = lax.dynamic_slice_in_dim(key_lists, me * blocks, blocks, 0)
    counts = lax.dynamic_slice_in_dim(key_counts, me * blocks, blocks, 0)
    sources = jnp.where(columns[None, :] < counts[:, None], mine // seg_dev, me).reshape(-1)
    entry = jnp.arange(blocks * MAXK, dtype=jnp.int32)
    same = sources[:, None] == sources[None, :]
    first = 1 - jnp.any(same & (entry[None, :] < entry[:, None]), axis=1).astype(jnp.int32)
    last = 1 - jnp.any(same & (entry[None, :] > entry[:, None]), axis=1).astype(jnp.int32)
    keys, values, stats, pieces = forward(
        sources, counts, fetched, queries_t, grad_out_t, w_key, w_value, grads
    )
    parts = exchange(pieces)
    ret, dq_t = backward(
        sources, counts, first, last, keys, values, queries, grad_out, queries_t, grad_out_t,
        stats, w_key.T, w_value.T, devices
    )
    ret = pl.pallas_call(
        finish_kernel,
        out_shape=jax.ShapeDtypeStruct(ret.shape, ret.dtype),
        in_specs=[ANY, ANY],
        out_specs=ANY,
        scratch_shapes=[
            pltpu.VMEM(parts.shape, BF16),
            pltpu.VMEM(parts.shape, BF16),
            pltpu.SemaphoreType.DMA,
        ],
        input_output_aliases={1: 0},
        compiler_params=pltpu.CompilerParams(vmem_limit_bytes=60 * MIB),
        name="finish",
    )(parts, ret)
    back = exchange(ret)
    base = dot(dq_t, w_query, 0, 1)
    grad_x, grad_w_out = pl.pallas_call(
        combine_kernel,
        out_shape=[
            jax.ShapeDtypeStruct((seg_dev, KEY_SEG, width), BF16),
            jax.ShapeDtypeStruct((width, width), F32),
        ],
        in_specs=[SMEM, ANY, VMEM],
        out_specs=[ANY, ANY],
        scratch_shapes=[
            pltpu.VMEM((devices, KEY_SEG * width // LANES, LANES), BF16),
            pltpu.VMEM((seg_dev, KEY_SEG, width), F32),
            pltpu.VMEM(parts.shape, BF16),
            pltpu.VMEM((width, width), F32),
            pltpu.VMEM((seg_dev, KEY_SEG, width), BF16),
            pltpu.SemaphoreType.DMA((devices,)),
            pltpu.SemaphoreType.DMA((3,)),
        ],
        compiler_params=pltpu.CompilerParams(vmem_limit_bytes=24 * MIB),
        name="combine",
    )(wanted, back, base.reshape(seg_dev, KEY_SEG, width))
    return grad_x.reshape(views_x.shape), grad_w_out


def solution(mesh):
    in_specs = (P("view", "row", None), P("view", "row", None), P(), P(), P(), P(), P(), P())
    out_specs = (P("view", "row", None), P())
    return jax.shard_map(local, mesh=mesh, in_specs=in_specs, out_specs=out_specs, check_vma=False)
```

```python
import jax
import jax.numpy as jnp
from jax import lax
from jax.experimental import pallas as pl
from jax.experimental.pallas import tpu as pltpu
from jax.sharding import PartitionSpec as P

HEAD_DIM = 64
QUERY_BLOCK = 128
KEY_SEG = 32
MAXK = 32
AXES = ("view", "row")
SPAN = MAXK * KEY_SEG
PAIR = 2 * HEAD_DIM
BOTH = 2 * QUERY_BLOCK
LANES = 128
MIB = 1024 * 1024
F32 = jnp.float32
BF16 = jnp.bfloat16
FWD_ROWS = 256
BWD_ROWS = 256
PROJ_ROWS = 256
PROJ_COLS = 256

def dot(a, b, ca=1, cb=0):
    return lax.dot_general(a, b, (((ca,), (cb,)), ((), ())), preferred_element_type=F32)

def split_heads(rows):
    low_half = lax.broadcasted_iota(jnp.int32, rows.shape, 1) < HEAD_DIM
    zero = jnp.zeros_like(rows)
    return jnp.concatenate(
        [jnp.where(low_half, rows, zero), jnp.where(low_half, zero, rows)], axis=0)

def split_channels(cols):
    zero = jnp.zeros((HEAD_DIM, QUERY_BLOCK), cols.dtype)
    return jnp.concatenate(
        [
            jnp.concatenate([cols[:HEAD_DIM], zero], axis=1),
            jnp.concatenate([zero, cols[HEAD_DIM:]], axis=1),
        ],
        axis=0,
    )


def fold(rows, op):
    return op(rows.reshape(rows.shape[0] // 8, 8, rows.shape[-1]), axis=0)

def masked_scores(k_rows, qb, live_rows, start):
    s = dot(k_rows, qb)
    ids = lax.broadcasted_iota(jnp.int32, s.shape, 0)
    return jnp.where(ids < live_rows - start, s, F32(-1e30))

def forward_kernel(
    sources, counts, x_hbm, qt_hbm, gt_hbm, wk_hbm, wv_hbm, dy_hbm,
    k_out, v_out, stat_ref, grad_ref,
    xg, ks, vs, ss, ps, att, qt_ref, gt_ref, wk_ref, wv_ref, dy_ref, sems, osems, wsems,
):
    blocks = qt_ref.shape[1] // QUERY_BLOCK
    width = x_hbm.shape[-1]
    pairs = width // PAIR

    def fetch(b):
        def one(j, carry):
            pltpu.make_async_copy(
                x_hbm.at[sources[b * MAXK + j]], xg.at[b * MAXK + j], sems.at[b]
            ).start()
            return carry
        lax.fori_loop(0, MAXK, one, 0, unroll=8)

    weights = [(wk_hbm, wk_ref), (wv_hbm, wv_ref), (qt_hbm, qt_ref), (gt_hbm, gt_ref), (dy_hbm, dy_ref)]
    loads = [pltpu.make_async_copy(a, z, wsems.at[i]) for i, (a, z) in enumerate(weights)]
    loads[0].start()
    loads[1].start()
    fetch(0)
    for load in loads[2:]:
        load.start()
    loads[0].wait()
    loads[1].wait()

    ncol = 2 * width // PROJ_COLS

    def project(b, c):
        if c == 0:
            mine = xg.at[pl.ds(b * MAXK, MAXK)]
            pltpu.make_async_copy(mine, mine, sems.at[b]).wait()
        half = ncol // 2
        w_ref, dst, hbm, sem = (
            (wk_ref, ks, k_out, osems.at[0]) if c < half else (wv_ref, vs, v_out, osems.at[1])
        )
        cols = pl.ds((c % half) * PROJ_COLS, PROJ_COLS)
        span = pl.ds(b * SPAN, SPAN)
        segs = PROJ_ROWS // KEY_SEG
        for r in range(SPAN // PROJ_ROWS):
            part = xg[pl.ds(b * MAXK + r * segs, segs)].reshape(PROJ_ROWS, width)
            dst[pl.ds(b * SPAN + r * PROJ_ROWS, PROJ_ROWS), cols] = dot(part, w_ref[:, cols]).astype(BF16)
        if c % half == half - 1:
            pltpu.make_async_copy(dst.at[span], hbm.at[span], sem).start()

    state = {}

    def scores(b, p):
        cols = pl.ds(p * PAIR, PAIR)
        tok = pl.ds(b * QUERY_BLOCK, QUERY_BLOCK)
        live_rows = counts[b] * KEY_SEG
        slot = (b * pairs + p) % 2
        qb = split_channels(qt_ref[cols, tok])
        state["top", b, p] = jnp.full((8, BOTH), -1e30, F32)

        def chunk(c):
            rows = pl.ds(c * FWD_ROWS, FWD_ROWS)
            s = masked_scores(ks[pl.ds(b * SPAN + c * FWD_ROWS, FWD_ROWS), cols], qb, live_rows, c * FWD_ROWS)
            ss[slot, rows, :] = s
            state["top", b, p] = jnp.maximum(state["top", b, p], fold(s, jnp.max))

        return [lambda c=c: chunk(c) for c in range(SPAN // FWD_ROWS)]

    def attend(b, p):
        slot = (b * pairs + p) % 2
        top = jnp.max(state["top", b, p], axis=0, keepdims=True)
        state["top", b, p] = top
        state["sum", b, p] = jnp.zeros((8, BOTH), F32)

        def chunk(c):
            rows = pl.ds(c * FWD_ROWS, FWD_ROWS)
            e = jnp.exp(ss[slot, rows, :] - top)
            ps[slot, rows, :] = e.astype(BF16)
            state["sum", b, p] = state["sum", b, p] + fold(e, jnp.sum)

        return [lambda c=c: chunk(c) for c in range(SPAN // FWD_ROWS)]

    def collect(b, p):
        cols = pl.ds(p * PAIR, PAIR)
        tok = pl.ds(b * QUERY_BLOCK, QUERY_BLOCK)
        slot = (b * pairs + p) % 2
        total = jnp.sum(state["sum", b, p], axis=0, keepdims=True)
        inverse = 1.0 / total
        out = dot(vs[pl.ds(b * SPAN, SPAN), cols], ps[slot], 0, 0)
        deltas = []
        for h in range(2):
            here = out[h * HEAD_DIM:(h + 1) * HEAD_DIM, h * QUERY_BLOCK:(h + 1) * QUERY_BLOCK]
            here = here * inverse[:, h * QUERY_BLOCK:(h + 1) * QUERY_BLOCK]
            here = here.astype(BF16)
            chan = pl.ds(p * PAIR + h * HEAD_DIM, HEAD_DIM)
            att[chan, tok] = here
            both = here.astype(F32) * gt_ref[chan, tok].astype(F32)
            deltas.append(jnp.sum(both, axis=0, keepdims=True))
        stat_ref[b, pl.ds(p, 1), :] = state["top", b, p] + jnp.log(total)
        stat_ref[b, pl.ds(pairs + p, 1), :] = jnp.concatenate(deltas, axis=1)

    for b in range(1, blocks):
        fetch(b)
    for c in range(ncol):
        project(0, c)
    for load in loads[2:]:
        load.wait()
    steps = [(b, p) for b in range(blocks) for p in range(pairs)]
    each = ncol // pairs
    for part in scores(*steps[0]):
        part()
    for i, (b, p) in enumerate(steps):
        more = []
        if i + 1 < len(steps):
            if p + 1 == pairs:
                for c in range((pairs - 1) * each, ncol):
                    project(b + 1, c)
            more = scores(*steps[i + 1])
        now = attend(b, p)
        for c in range(len(now)):
            if more and c < len(more):
                more[c]()
            now[c]()
        if b + 1 < blocks and p + 1 < pairs:
            for c in range(p * each, (p + 1) * each):
                project(b + 1, c)
        collect(b, p)
    per = grad_ref.shape[1]
    slots = width // LANES
    for r in range(width // 128):
        g = dot(att[pl.ds(r * 128, 128), :], dy_ref[...]).astype(BF16)
        for i in range(128 // per):
            for t in range(slots):
                grad_ref[(r * (128 // per) + i) * slots + t] = g[
                    i * per:(i + 1) * per, t * LANES:(t + 1) * LANES
                ]
    pltpu.make_async_copy(ks, k_out, osems.at[0]).wait()
    pltpu.make_async_copy(vs, v_out, osems.at[1]).wait()


def backward_kernel(
    sources, counts, first, last, k_hbm, v_hbm, q_hbm, g_hbm, qt_hbm, gt_hbm, stat_ref, wk_hbm, wv_hbm,
    ret_hbm, dq_ref,
    ks, vs, ps, ds, dkv, acc, q_ref, g_ref, qt_ref, gt_ref, w_ref, out, sems, wsems, osem,
):
    blocks = q_ref.shape[0] // QUERY_BLOCK
    width = w_ref.shape[-1]
    pairs = width // PAIR
    devices = acc.shape[0]
    weights = [
        (qt_hbm, qt_ref), (gt_hbm, gt_ref), (q_hbm, q_ref), (g_hbm, g_ref),
        (wk_hbm, w_ref.at[pl.ds(0, width)]), (wv_hbm, w_ref.at[pl.ds(width, width)]),
    ]
    loads = [pltpu.make_async_copy(a, z, wsems.at[i]) for i, (a, z) in enumerate(weights)]

    def fetch(b):
        span = pl.ds(b * SPAN, SPAN)
        pltpu.make_async_copy(k_hbm.at[span], ks.at[span], sems.at[b, 0]).start()
        pltpu.make_async_copy(v_hbm.at[span], vs.at[span], sems.at[b, 1]).start()

    loads[0].start()
    loads[1].start()
    fetch(0)
    for load in loads[2:]:
        load.start()
    for b in range(1, blocks):
        fetch(b)
    loads[0].wait()
    loads[1].wait()

    def soft(b, p):
        if p == 0:
            span = pl.ds(b * SPAN, SPAN)
            pltpu.make_async_copy(ks.at[span], ks.at[span], sems.at[b, 0]).wait()
            pltpu.make_async_copy(vs.at[span], vs.at[span], sems.at[b, 1]).wait()
        tok = pl.ds(b * QUERY_BLOCK, QUERY_BLOCK)
        live_rows = counts[b] * KEY_SEG
        slot = (b * pairs + p) % 2
        cols = pl.ds(p * PAIR, PAIR)
        qb = split_channels(qt_ref[cols, tok])
        gb = split_channels(gt_ref[cols, tok])
        lse = stat_ref[b, pl.ds(p, 1), :]
        delta = stat_ref[b, pl.ds(pairs + p, 1), :]

        def chunk(c):
            rows = pl.ds(c * BWD_ROWS, BWD_ROWS)
            there = pl.ds(b * SPAN + c * BWD_ROWS, BWD_ROWS)
            s = masked_scores(ks[there, cols], qb, live_rows, c * BWD_ROWS)
            dp = dot(vs[there, cols], gb)
            w = jnp.exp(s - lse)
            ps[slot, rows, :] = w.astype(BF16)
            ds[slot, rows, :] = (w * (dp - delta)).astype(BF16)

        return [lambda c=c: chunk(c) for c in range(SPAN // BWD_ROWS)]

    def grads(b, p):
        tok = pl.ds(b * QUERY_BLOCK, QUERY_BLOCK)
        slot = (b * pairs + p) % 2
        cols = pl.ds(p * PAIR, PAIR)
        qb = split_heads(q_ref[tok, cols])
        gb = split_heads(g_ref[tok, cols])

        def do_dv():
            dkv[b % 2, :, pl.ds(width + p * PAIR, PAIR)] = dot(ps[slot], gb).astype(BF16)

        def do_dk():
            dkv[b % 2, :, cols] = dot(ds[slot], qb).astype(BF16)

        def do_dq():
            dq = dot(ks[pl.ds(b * SPAN, SPAN), cols], ds[slot], 0, 0) * F32(HEAD_DIM ** -0.5)
            for h in range(2):
                here = dq[h * HEAD_DIM:(h + 1) * HEAD_DIM, h * QUERY_BLOCK:(h + 1) * QUERY_BLOCK]
                dq_ref[pl.ds(p * PAIR + h * HEAD_DIM, HEAD_DIM), tok] = here.astype(BF16)

        return [do_dv, do_dk, do_dq]

    lines = KEY_SEG * width // LANES
    per = SPAN // pairs
    segs = per // KEY_SEG

    def back(b, c):
        rows = pl.ds(c * per, per)
        term = dot(dkv[b % 2, rows, :], w_ref[...])
        for j in range(segs):
            entry = b * MAXK + c * segs + j
            slot = sources[entry]
            mine = term[j * KEY_SEG:(j + 1) * KEY_SEG, :]
            if b:
                mine = jnp.where(first[entry] > 0, mine, acc[slot] + mine)
            if b + 1 < blocks:
                acc[slot] = mine
            low = mine.astype(BF16)
            for u in range(width // LANES):
                out[slot, pl.ds(u * KEY_SEG, KEY_SEG), :] = low[:, u * LANES:(u + 1) * LANES]

    def line(entry):
        slot = sources[entry]
        return pltpu.make_async_copy(out.at[slot], ret_hbm.at[slot, pl.ds(0, lines)], osem)

    def send(start, size):
        def one(entry, carry):
            @pl.when(last[entry] > 0)
            def _():
                line(entry).start()

            return carry

        lax.fori_loop(start, start + size, one, 0, unroll=4)

    steps = [(b, p) for b in range(blocks) for p in range(pairs)]
    for i in range(len(steps) + 1):
        now = soft(*steps[i]) if i < len(steps) else []
        if i == 1:
            loads[2].wait()
            loads[3].wait()
        old = grads(*steps[i - 1]) if i else []
        for c in range(max(len(now), len(old))):
            if c < len(now):
                now[c]()
            if c < len(old):
                old[c]()
        if i == 1:
            for load in loads[4:]:
                load.wait()
        if i and steps[i - 1][0]:
            back(steps[i - 1][0] - 1, steps[i - 1][1])
            if steps[i - 1][1] == pairs - 1:
                send((steps[i - 1][0] - 1) * MAXK, MAXK)
    for p in range(pairs):
        back(blocks - 1, p)
        send((blocks - 1) * MAXK + p * segs, segs)

    def finish(entry, carry):
        @pl.when(last[entry] > 0)
        def _():
            line(entry).wait()

        return carry

    lax.fori_loop(0, blocks * MAXK, finish, 0, unroll=4)


VMEM = pl.BlockSpec(memory_space=pltpu.VMEM)
SMEM = pl.BlockSpec(memory_space=pltpu.SMEM)
ANY = pl.BlockSpec(memory_space=pl.ANY)

def square(width, tokens):
    return pltpu.VMEM((tokens, width), BF16)

def forward(sources, counts, fetched, queries_t, grad_out_t, w_key, w_value, grads):
    devices, _, width = fetched.shape
    tokens = queries_t.shape[1]
    blocks = tokens // QUERY_BLOCK
    keys = blocks * SPAN
    per = width * width // (devices * LANES)
    return pl.pallas_call(
        forward_kernel,
        out_shape=[
            jax.ShapeDtypeStruct((keys, width), BF16),
            jax.ShapeDtypeStruct((keys, width), BF16),
            jax.ShapeDtypeStruct((blocks, 2 * width // PAIR, BOTH), F32),
            jax.ShapeDtypeStruct((devices, per, LANES), BF16),
        ],
        in_specs=[SMEM, SMEM] + [ANY] * 6,
        out_specs=[ANY, ANY, VMEM, VMEM],
        scratch_shapes=[
            pltpu.VMEM((blocks * MAXK, KEY_SEG, width), BF16),
            pltpu.VMEM((keys, width), BF16),
            pltpu.VMEM((keys, width), BF16),
            pltpu.VMEM((2, SPAN, BOTH), F32),
            pltpu.VMEM((2, SPAN, BOTH), BF16),
            pltpu.VMEM((width, tokens), BF16),
            pltpu.VMEM((tokens, width), BF16),
            pltpu.VMEM((width, tokens), BF16),
            pltpu.VMEM((width, width), BF16),
            pltpu.VMEM((width, width), BF16),
            pltpu.VMEM((tokens, width), BF16),
            pltpu.SemaphoreType.DMA((blocks,)),
            pltpu.SemaphoreType.DMA((2,)),
            pltpu.SemaphoreType.DMA((5,)),
        ],
        compiler_params=pltpu.CompilerParams(vmem_limit_bytes=60 * MIB),
        cost_estimate=pl.CostEstimate(
            flops=10_000_000_000, bytes_accessed=8 * MIB, transcendentals=4 * MIB),
        name="forward",
    )(sources, counts, fetched, queries_t, grad_out_t, w_key, w_value, grads)


def backward(sources, counts, first, last, keys, values, queries, grad_out, queries_t, grad_out_t, stats, w_key, w_value, devices):
    tokens, width = queries.shape
    blocks = tokens // QUERY_BLOCK
    lines = KEY_SEG * width // LANES
    extra = width * width // (devices * LANES)
    return pl.pallas_call(
        backward_kernel,
        out_shape=[
            jax.ShapeDtypeStruct((devices, lines + extra, LANES), BF16),
            jax.ShapeDtypeStruct((width, tokens), BF16),
        ],
        in_specs=[SMEM] * 4 + [ANY] * 6 + [VMEM] + [ANY] * 2,
        out_specs=[ANY, VMEM],
        scratch_shapes=[
            pltpu.VMEM((blocks * SPAN, width), BF16),
            pltpu.VMEM((blocks * SPAN, width), BF16),
            pltpu.VMEM((2, SPAN, BOTH), BF16),
            pltpu.VMEM((2, SPAN, BOTH), BF16),
            pltpu.VMEM((2, SPAN, 2 * width), BF16),
            pltpu.VMEM((devices, KEY_SEG, width), F32),
            pltpu.VMEM((tokens, width), BF16),
            pltpu.VMEM((tokens, width), BF16),
            pltpu.VMEM((width, tokens), BF16),
            pltpu.VMEM((width, tokens), BF16),
            pltpu.VMEM((2 * width, width), BF16),
            pltpu.VMEM((devices, lines, LANES), BF16),
            pltpu.SemaphoreType.DMA((blocks, 2)),
            pltpu.SemaphoreType.DMA((6,)),
            pltpu.SemaphoreType.DMA,
        ],
        compiler_params=pltpu.CompilerParams(vmem_limit_bytes=60 * MIB),
        cost_estimate=pl.CostEstimate(
            flops=20_000_000_000, bytes_accessed=16 * MIB, transcendentals=4 * MIB),
        name="backward",
              )(sources, counts, first, last, keys, values, queries, grad_out, queries_t, grad_out_t, stats, w_key, w_value)


def gather_kernel(wanted, x_hbm, out_ref, x_ref, sems):
    load = pltpu.make_async_copy(x_hbm, x_ref, sems.at[0])
    load.start()
    load.wait()

    def step(i, carry):
        pltpu.make_async_copy(
            x_ref.at[jnp.maximum(wanted[i], 0)], out_ref.at[i], sems.at[1]
        ).start()
        return carry

    lax.fori_loop(0, out_ref.shape[0], step, 0, unroll=8)
    pltpu.make_async_copy(out_ref, out_ref, sems.at[1]).wait()


def finish_kernel(part_ref, ret_in, ret_out, wide, sem):
    wide[...] = jnp.broadcast_to(part_ref[...][None], wide.shape)
    extra = wide.shape[1]
    rows = pl.ds(ret_out.shape[1] - extra, extra)
    copy = pltpu.make_async_copy(wide, ret_out.at[:, rows], sem)
    copy.start()
    copy.wait()


def combine_kernel(wanted, back_hbm, base_ref, out_hbm, grad_hbm, back, acc, grad, out, sems, ends):
    devices, lines, _ = back.shape
    groups = sems.shape[0]
    size = devices // groups
    width = base_ref.shape[-1]
    slots = width // LANES
    extra = lines - KEY_SEG * slots
    tall = size // slots * extra

    def copy(t):
        part = pl.ds(t * size, size)
        return pltpu.make_async_copy(back_hbm.at[part], back.at[part], sems.at[t])

    for t in range(groups):
        copy(t).start()
    acc[...] = base_ref[...]
    for t in range(groups):
        copy(t).wait()
        for i in range(t * size, (t + 1) * size):
            rows = pl.ds((i // slots) * extra, extra)
            cols = pl.ds((i % slots) * LANES, LANES)
            grad[rows, cols] = back[i, pl.ds(lines - extra, extra), :].astype(F32)
        part = pl.ds(t * tall, tall)
        pltpu.make_async_copy(grad.at[part], grad_hbm.at[part], ends.at[0]).start()

        def step(i, carry):
            seg = wanted[i]

            @pl.when(seg >= 0)
            def _():
                for u in range(slots):
                    cols = pl.ds(u * LANES, LANES)
                    acc[seg, :, cols] += back[i, pl.ds(u * KEY_SEG, KEY_SEG), :].astype(F32)

            return carry

        lax.fori_loop(t * size, (t + 1) * size, step, 0)
    out[...] = acc[...].astype(out.dtype)
    last = pltpu.make_async_copy(out, out_hbm, ends.at[1])
    last.start()
    pltpu.make_async_copy(grad, grad_hbm, ends.at[0]).wait()
    last.wait()


def exchange(v):
    return lax.all_to_all(v, AXES, split_axis=0, concat_axis=0, tiled=True)


def local(views_x, dy, w_query, w_key, w_value, w_out, key_lists, key_counts):
    width = views_x.shape[-1]
    x = views_x.reshape(-1, width)
    grads = dy.reshape(-1, width)
    tokens = x.shape[0]
    devices = lax.axis_size(AXES)
    me = lax.axis_index(AXES)
    seg_dev = tokens // KEY_SEG
    blocks = tokens // QUERY_BLOCK
    columns = jnp.arange(MAXK, dtype=jnp.int32)
    live = columns[None, :] < key_counts[:, None]
    asked = live & (key_lists // seg_dev == me)
    wanted = jnp.max(
        jnp.where(asked, key_lists % seg_dev, -1).reshape(devices, blocks * MAXK), axis=1
    )
    outgoing = pl.pallas_call(
        gather_kernel,
        out_shape=jax.ShapeDtypeStruct((devices, KEY_SEG, width), BF16),
        in_specs=[SMEM, ANY],
        out_specs=ANY,
        scratch_shapes=[
            pltpu.VMEM((seg_dev, KEY_SEG, width), BF16),
            pltpu.SemaphoreType.DMA((2,)),
        ],
        name="gather",
    )(wanted, x.reshape(seg_dev, KEY_SEG, width))
    fetched = exchange(outgoing)

    queries = dot(x, w_query).astype(BF16) * BF16(HEAD_DIM ** -0.5)
    grad_out = dot(grads, w_out, 1, 1).astype(BF16)
    queries_t = queries.T
    grad_out_t = grad_out.T
    mine = lax.dynamic_slice_in_dim(key_lists, me * blocks, blocks, 0)
    counts = lax.dynamic_slice_in_dim(key_counts, me * blocks, blocks, 0)
    sources = jnp.where(columns[None, :] < counts[:, None], mine // seg_dev, me).reshape(-1)
    entry = jnp.arange(blocks * MAXK, dtype=jnp.int32)
    same = sources[:, None] == sources[None, :]
    first = 1 - jnp.any(same & (entry[None, :] < entry[:, None]), axis=1).astype(jnp.int32)
    last = 1 - jnp.any(same & (entry[None, :] > entry[:, None]), axis=1).astype(jnp.int32)
    keys, values, stats, pieces = forward(
        sources, counts, fetched, queries_t, grad_out_t, w_key, w_value, grads
    )
    parts = exchange(pieces)
    ret, dq_t = backward(
        sources, counts, first, last, keys, values, queries, grad_out, queries_t, grad_out_t,
        stats, w_key.T, w_value.T, devices
    )
    part = jnp.sum(parts.astype(F32), axis=0).astype(BF16)
    ret = pl.pallas_call(
        finish_kernel,
        out_shape=jax.ShapeDtypeStruct(ret.shape, ret.dtype),
        in_specs=[VMEM, ANY],
        out_specs=ANY,
        scratch_shapes=[pltpu.VMEM(parts.shape, BF16), pltpu.SemaphoreType.DMA],
        input_output_aliases={1: 0},
        compiler_params=pltpu.CompilerParams(vmem_limit_bytes=57 * MIB),
        name="finish",
    )(part, ret)
    back = exchange(ret)
    base = dot(dq_t, w_query, 0, 1)
    grad_x, grad_w_out = pl.pallas_call(
        combine_kernel,
        out_shape=[
            jax.ShapeDtypeStruct((seg_dev, KEY_SEG, width), BF16),
            jax.ShapeDtypeStruct((width, width), F32),
        ],
        in_specs=[SMEM, ANY, VMEM],
        out_specs=[ANY, ANY],
        scratch_shapes=[
            pltpu.VMEM(ret.shape, BF16),
            pltpu.VMEM((seg_dev, KEY_SEG, width), F32),
            pltpu.VMEM((width, width), F32),
            pltpu.VMEM((seg_dev, KEY_SEG, width), BF16),
            pltpu.SemaphoreType.DMA((8,)),
            pltpu.SemaphoreType.DMA((2,)),
        ],
        compiler_params=pltpu.CompilerParams(vmem_limit_bytes=24 * MIB),
        name="combine",
    )(wanted, back, base.reshape(seg_dev, KEY_SEG, width))
    return grad_x.reshape(views_x.shape), grad_w_out


def solution(mesh):
    in_specs = (P("view", "row", None), P("view", "row", None), P(), P(), P(), P(), P(), P())
    out_specs = (P("view", "row", None), P())
    return jax.shard_map(local, mesh=mesh, in_specs=in_specs, out_specs=out_specs, check_vma=False)
```

```python
import jax
import jax.numpy as jnp
from jax import lax
from jax.experimental import pallas as pl
from jax.experimental.pallas import tpu as pltpu
from jax.sharding import PartitionSpec as P

HEAD_DIM = 64
QUERY_BLOCK = 128
KEY_SEG = 32
MAXK = 32
AXES = ("view", "row")
SPAN = MAXK * KEY_SEG
PAIR = 2 * HEAD_DIM
BOTH = 2 * QUERY_BLOCK
LANES = 128
MIB = 1024 * 1024
F32 = jnp.float32
BF16 = jnp.bfloat16
FWD_ROWS = 256
BWD_ROWS = 256
PROJ_ROWS = 256
PROJ_COLS = 256

def dot(a, b, ca=1, cb=0):
    return lax.dot_general(a, b, (((ca,), (cb,)), ((), ())), preferred_element_type=F32)

def split_heads(rows):
    low_half = lax.broadcasted_iota(jnp.int32, rows.shape, 1) < HEAD_DIM
    zero = jnp.zeros_like(rows)
    return jnp.concatenate(
        [jnp.where(low_half, rows, zero), jnp.where(low_half, zero, rows)], axis=0)

def split_channels(cols):
    zero = jnp.zeros((HEAD_DIM, QUERY_BLOCK), cols.dtype)
    return jnp.concatenate(
        [
            jnp.concatenate([cols[:HEAD_DIM], zero], axis=1),
            jnp.concatenate([zero, cols[HEAD_DIM:]], axis=1),
        ],
        axis=0,
    )


def fold(rows, op):
    return op(rows.reshape(rows.shape[0] // 8, 8, rows.shape[-1]), axis=0)

def masked_scores(k_rows, qb, live_rows, start):
    s = dot(k_rows, qb)
    ids = lax.broadcasted_iota(jnp.int32, s.shape, 0)
    return jnp.where(ids < live_rows - start, s, F32(-1e30))

def forward_kernel(
    sources, counts, x_hbm, qt_hbm, gt_hbm, wk_hbm, wv_hbm, dy_hbm,
    k_out, v_out, stat_ref, grad_ref,
    xg, ks, vs, ss, ps, att, qt_ref, gt_ref, wk_ref, wv_ref, dy_ref, sems, osems, wsems,
):
    blocks = qt_ref.shape[1] // QUERY_BLOCK
    width = x_hbm.shape[-1]
    pairs = width // PAIR

    def fetch(b):
        def one(j, carry):
            pltpu.make_async_copy(
                x_hbm.at[sources[b * MAXK + j]], xg.at[b * MAXK + j], sems.at[b]
            ).start()
            return carry
        lax.fori_loop(0, MAXK, one, 0, unroll=8)

    weights = [(wk_hbm, wk_ref), (wv_hbm, wv_ref), (qt_hbm, qt_ref), (gt_hbm, gt_ref), (dy_hbm, dy_ref)]
    loads = [pltpu.make_async_copy(a, z, wsems.at[i]) for i, (a, z) in enumerate(weights)]
    loads[0].start()
    loads[1].start()
    fetch(0)
    for load in loads[2:]:
        load.start()
    loads[0].wait()
    loads[1].wait()

    ncol = 2 * width // PROJ_COLS

    def project(b, c):
        if c == 0:
            mine = xg.at[pl.ds(b * MAXK, MAXK)]
            pltpu.make_async_copy(mine, mine, sems.at[b]).wait()
        half = ncol // 2
        w_ref, dst, hbm, sem = (
            (wk_ref, ks, k_out, osems.at[0]) if c < half else (wv_ref, vs, v_out, osems.at[1])
        )
        cols = pl.ds((c % half) * PROJ_COLS, PROJ_COLS)
        span = pl.ds(b * SPAN, SPAN)
        segs = PROJ_ROWS // KEY_SEG
        for r in range(SPAN // PROJ_ROWS):
            part = xg[pl.ds(b * MAXK + r * segs, segs)].reshape(PROJ_ROWS, width)
            dst[pl.ds(b * SPAN + r * PROJ_ROWS, PROJ_ROWS), cols] = dot(part, w_ref[:, cols]).astype(BF16)
        if c % half == half - 1:
            pltpu.make_async_copy(dst.at[span], hbm.at[span], sem).start()

    state = {}

    def scores(b, p):
        cols = pl.ds(p * PAIR, PAIR)
        tok = pl.ds(b * QUERY_BLOCK, QUERY_BLOCK)
        live_rows = counts[b] * KEY_SEG
        slot = (b * pairs + p) % 2
        qb = split_channels(qt_ref[cols, tok])
        state["top", b, p] = jnp.full((8, BOTH), -1e30, F32)

        def chunk(c):
            rows = pl.ds(c * FWD_ROWS, FWD_ROWS)
            s = masked_scores(ks[pl.ds(b * SPAN + c * FWD_ROWS, FWD_ROWS), cols], qb, live_rows, c * FWD_ROWS)
            ss[slot, rows, :] = s
            state["top", b, p] = jnp.maximum(state["top", b, p], fold(s, jnp.max))

        return [lambda c=c: chunk(c) for c in range(SPAN // FWD_ROWS)]

    def attend(b, p):
        slot = (b * pairs + p) % 2
        top = jnp.max(state["top", b, p], axis=0, keepdims=True)
        state["top", b, p] = top
        state["sum", b, p] = jnp.zeros((8, BOTH), F32)

        def chunk(c):
            rows = pl.ds(c * FWD_ROWS, FWD_ROWS)
            e = jnp.exp(ss[slot, rows, :] - top)
            ps[slot, rows, :] = e.astype(BF16)
            state["sum", b, p] = state["sum", b, p] + fold(e, jnp.sum)

        return [lambda c=c: chunk(c) for c in range(SPAN // FWD_ROWS)]

    def collect(b, p):
        cols = pl.ds(p * PAIR, PAIR)
        tok = pl.ds(b * QUERY_BLOCK, QUERY_BLOCK)
        slot = (b * pairs + p) % 2
        total = jnp.sum(state["sum", b, p], axis=0, keepdims=True)
        inverse = 1.0 / total
        out = dot(vs[pl.ds(b * SPAN, SPAN), cols], ps[slot], 0, 0)
        deltas = []
        for h in range(2):
            here = out[h * HEAD_DIM:(h + 1) * HEAD_DIM, h * QUERY_BLOCK:(h + 1) * QUERY_BLOCK]
            here = here * inverse[:, h * QUERY_BLOCK:(h + 1) * QUERY_BLOCK]
            here = here.astype(BF16)
            chan = pl.ds(p * PAIR + h * HEAD_DIM, HEAD_DIM)
            att[chan, tok] = here
            both = here.astype(F32) * gt_ref[chan, tok].astype(F32)
            deltas.append(jnp.sum(both, axis=0, keepdims=True))
        stat_ref[b, pl.ds(p, 1), :] = state["top", b, p] + jnp.log(total)
        stat_ref[b, pl.ds(pairs + p, 1), :] = jnp.concatenate(deltas, axis=1)

    for b in range(1, blocks):
        fetch(b)
    for c in range(ncol):
        project(0, c)
    for load in loads[2:]:
        load.wait()
    steps = [(b, p) for b in range(blocks) for p in range(pairs)]
    each = ncol // pairs
    for part in scores(*steps[0]):
        part()
    for i, (b, p) in enumerate(steps):
        more = []
        if i + 1 < len(steps):
            if p + 1 == pairs:
                for c in range((pairs - 1) * each, ncol):
                    project(b + 1, c)
            more = scores(*steps[i + 1])
        now = attend(b, p)
        for c in range(len(now)):
            if more and c < len(more):
                more[c]()
            now[c]()
        if b + 1 < blocks and p + 1 < pairs:
            for c in range(p * each, (p + 1) * each):
                project(b + 1, c)
        collect(b, p)
    per = grad_ref.shape[1]
    slots = width // LANES
    for r in range(width // 128):
        g = dot(att[pl.ds(r * 128, 128), :], dy_ref[...]).astype(BF16)
        for i in range(128 // per):
            for t in range(slots):
                grad_ref[(r * (128 // per) + i) * slots + t] = g[
                    i * per:(i + 1) * per, t * LANES:(t + 1) * LANES
                ]
    pltpu.make_async_copy(ks, k_out, osems.at[0]).wait()
    pltpu.make_async_copy(vs, v_out, osems.at[1]).wait()


def backward_kernel(
    sources, counts, first, last, k_hbm, v_hbm, q_hbm, g_hbm, qt_hbm, gt_hbm, stat_ref, wk_hbm, wv_hbm,
    ret_hbm, dq_ref,
    ks, vs, ps, ds, dk, dv, acc, q_ref, g_ref, qt_ref, gt_ref, wk_ref, wv_ref, out, sems, wsems, osem,
):
    blocks = q_ref.shape[0] // QUERY_BLOCK
    width = wk_ref.shape[-1]
    pairs = width // PAIR
    devices = acc.shape[0]
    weights = [
        (qt_hbm, qt_ref), (gt_hbm, gt_ref), (q_hbm, q_ref), (g_hbm, g_ref),
        (wk_hbm, wk_ref), (wv_hbm, wv_ref),
    ]
    loads = [pltpu.make_async_copy(a, z, wsems.at[i]) for i, (a, z) in enumerate(weights)]

    def fetch(b):
        span = pl.ds(b * SPAN, SPAN)
        pltpu.make_async_copy(k_hbm.at[span], ks.at[span], sems.at[b, 0]).start()
        pltpu.make_async_copy(v_hbm.at[span], vs.at[span], sems.at[b, 1]).start()

    loads[0].start()
    loads[1].start()
    fetch(0)
    for load in loads[2:]:
        load.start()
    for b in range(1, blocks):
        fetch(b)
    loads[0].wait()
    loads[1].wait()

    def soft(b, p):
        if p == 0:
            span = pl.ds(b * SPAN, SPAN)
            pltpu.make_async_copy(ks.at[span], ks.at[span], sems.at[b, 0]).wait()
            pltpu.make_async_copy(vs.at[span], vs.at[span], sems.at[b, 1]).wait()
        tok = pl.ds(b * QUERY_BLOCK, QUERY_BLOCK)
        live_rows = counts[b] * KEY_SEG
        slot = (b * pairs + p) % 2
        cols = pl.ds(p * PAIR, PAIR)
        qb = split_channels(qt_ref[cols, tok])
        gb = split_channels(gt_ref[cols, tok])
        lse = stat_ref[b, pl.ds(p, 1), :]
        delta = stat_ref[b, pl.ds(pairs + p, 1), :]

        def chunk(c):
            rows = pl.ds(c * BWD_ROWS, BWD_ROWS)
            there = pl.ds(b * SPAN + c * BWD_ROWS, BWD_ROWS)
            s = masked_scores(ks[there, cols], qb, live_rows, c * BWD_ROWS)
            dp = dot(vs[there, cols], gb)
            w = jnp.exp(s - lse)
            ps[slot, rows, :] = w.astype(BF16)
            ds[slot, rows, :] = (w * (dp - delta)).astype(BF16)

        return [lambda c=c: chunk(c) for c in range(SPAN // BWD_ROWS)]

    def grads(b, p):
        tok = pl.ds(b * QUERY_BLOCK, QUERY_BLOCK)
        slot = (b * pairs + p) % 2
        cols = pl.ds(p * PAIR, PAIR)
        qb = split_heads(q_ref[tok, cols])
        gb = split_heads(g_ref[tok, cols])

        def do_dv():
            dv[b % 2, :, cols] = dot(ps[slot], gb).astype(BF16)

        def do_dk():
            dk[b % 2, :, cols] = dot(ds[slot], qb).astype(BF16)

        def do_dq():
            dq = dot(ks[pl.ds(b * SPAN, SPAN), cols], ds[slot], 0, 0) * F32(HEAD_DIM ** -0.5)
            for h in range(2):
                here = dq[h * HEAD_DIM:(h + 1) * HEAD_DIM, h * QUERY_BLOCK:(h + 1) * QUERY_BLOCK]
                dq_ref[pl.ds(p * PAIR + h * HEAD_DIM, HEAD_DIM), tok] = here.astype(BF16)

        return [do_dv, do_dk, do_dq]

    lines = KEY_SEG * width // LANES
    per = SPAN // pairs
    segs = per // KEY_SEG

    def back(b, c):
        rows = pl.ds(c * per, per)
        term = dot(dk[b % 2, rows, :], wk_ref[...]) + dot(dv[b % 2, rows, :], wv_ref[...])
        for j in range(segs):
            entry = b * MAXK + c * segs + j
            slot = sources[entry]
            mine = term[j * KEY_SEG:(j + 1) * KEY_SEG, :]
            if b:
                mine = jnp.where(first[entry] > 0, mine, acc[slot] + mine)
            if b + 1 < blocks:
                acc[slot] = mine
            low = mine.astype(BF16)
            for u in range(width // LANES):
                out[slot, pl.ds(u * KEY_SEG, KEY_SEG), :] = low[:, u * LANES:(u + 1) * LANES]

    def line(entry):
        slot = sources[entry]
        return pltpu.make_async_copy(out.at[slot], ret_hbm.at[slot, pl.ds(0, lines)], osem)

    def send(start, size):
        def one(entry, carry):
            @pl.when(last[entry] > 0)
            def _():
                line(entry).start()

            return carry

        lax.fori_loop(start, start + size, one, 0, unroll=4)

    steps = [(b, p) for b in range(blocks) for p in range(pairs)]
    for i in range(len(steps) + 1):
        now = soft(*steps[i]) if i < len(steps) else []
        if i == 1:
            loads[2].wait()
            loads[3].wait()
        old = grads(*steps[i - 1]) if i else []
        for c in range(max(len(now), len(old))):
            if c < len(now):
                now[c]()
            if c < len(old):
                old[c]()
        if i == 1:
            for load in loads[4:]:
                load.wait()
        if i and steps[i - 1][0]:
            back(steps[i - 1][0] - 1, steps[i - 1][1])
            if steps[i - 1][1] == pairs - 1:
                send((steps[i - 1][0] - 1) * MAXK, MAXK)
    for p in range(pairs):
        back(blocks - 1, p)
        send((blocks - 1) * MAXK + p * segs, segs)

    def finish(entry, carry):
        @pl.when(last[entry] > 0)
        def _():
            line(entry).wait()

        return carry

    lax.fori_loop(0, blocks * MAXK, finish, 0, unroll=4)


VMEM = pl.BlockSpec(memory_space=pltpu.VMEM)
SMEM = pl.BlockSpec(memory_space=pltpu.SMEM)
ANY = pl.BlockSpec(memory_space=pl.ANY)

def square(width, tokens):
    return pltpu.VMEM((tokens, width), BF16)

def forward(sources, counts, fetched, queries_t, grad_out_t, w_key, w_value, grads):
    devices, _, width = fetched.shape
    tokens = queries_t.shape[1]
    blocks = tokens // QUERY_BLOCK
    keys = blocks * SPAN
    per = width * width // (devices * LANES)
    return pl.pallas_call(
        forward_kernel,
        out_shape=[
            jax.ShapeDtypeStruct((keys, width), BF16),
            jax.ShapeDtypeStruct((keys, width), BF16),
            jax.ShapeDtypeStruct((blocks, 2 * width // PAIR, BOTH), F32),
            jax.ShapeDtypeStruct((devices, per, LANES), BF16),
        ],
        in_specs=[SMEM, SMEM] + [ANY] * 6,
        out_specs=[ANY, ANY, VMEM, VMEM],
        scratch_shapes=[
            pltpu.VMEM((blocks * MAXK, KEY_SEG, width), BF16),
            pltpu.VMEM((keys, width), BF16),
            pltpu.VMEM((keys, width), BF16),
            pltpu.VMEM((2, SPAN, BOTH), F32),
            pltpu.VMEM((2, SPAN, BOTH), BF16),
            pltpu.VMEM((width, tokens), BF16),
            pltpu.VMEM((tokens, width), BF16),
            pltpu.VMEM((width, tokens), BF16),
            pltpu.VMEM((width, width), BF16),
            pltpu.VMEM((width, width), BF16),
            pltpu.VMEM((tokens, width), BF16),
            pltpu.SemaphoreType.DMA((blocks,)),
            pltpu.SemaphoreType.DMA((2,)),
            pltpu.SemaphoreType.DMA((5,)),
        ],
        compiler_params=pltpu.CompilerParams(vmem_limit_bytes=60 * MIB),
        cost_estimate=pl.CostEstimate(
            flops=10_000_000_000, bytes_accessed=8 * MIB, transcendentals=4 * MIB),
        name="forward",
    )(sources, counts, fetched, queries_t, grad_out_t, w_key, w_value, grads)


def backward(sources, counts, first, last, keys, values, queries, grad_out, queries_t, grad_out_t, stats, w_key, w_value, devices):
    tokens, width = queries.shape
    blocks = tokens // QUERY_BLOCK
    lines = KEY_SEG * width // LANES
    extra = width * width // (devices * LANES)
    return pl.pallas_call(
        backward_kernel,
        out_shape=[
            jax.ShapeDtypeStruct((devices, lines + extra, LANES), BF16),
            jax.ShapeDtypeStruct((width, tokens), BF16),
        ],
        in_specs=[SMEM] * 4 + [ANY] * 6 + [VMEM] + [ANY] * 2,
        out_specs=[ANY, VMEM],
        scratch_shapes=[
            pltpu.VMEM((blocks * SPAN, width), BF16),
            pltpu.VMEM((blocks * SPAN, width), BF16),
            pltpu.VMEM((2, SPAN, BOTH), BF16),
            pltpu.VMEM((2, SPAN, BOTH), BF16),
            pltpu.VMEM((2, SPAN, width), BF16),
            pltpu.VMEM((2, SPAN, width), BF16),
            pltpu.VMEM((devices, KEY_SEG, width), F32),
            pltpu.VMEM((tokens, width), BF16),
            pltpu.VMEM((tokens, width), BF16),
            pltpu.VMEM((width, tokens), BF16),
            pltpu.VMEM((width, tokens), BF16),
            pltpu.VMEM((width, width), BF16),
            pltpu.VMEM((width, width), BF16),
            pltpu.VMEM((devices, lines, LANES), BF16),
            pltpu.SemaphoreType.DMA((blocks, 2)),
            pltpu.SemaphoreType.DMA((6,)),
            pltpu.SemaphoreType.DMA,
        ],
        compiler_params=pltpu.CompilerParams(vmem_limit_bytes=60 * MIB),
        cost_estimate=pl.CostEstimate(
            flops=20_000_000_000, bytes_accessed=16 * MIB, transcendentals=4 * MIB),
        name="backward",
              )(sources, counts, first, last, keys, values, queries, grad_out, queries_t, grad_out_t, stats, w_key, w_value)


def gather_kernel(wanted, x_hbm, out_ref, x_ref, sems):
    load = pltpu.make_async_copy(x_hbm, x_ref, sems.at[0])
    load.start()
    load.wait()

    def step(i, carry):
        pltpu.make_async_copy(
            x_ref.at[jnp.maximum(wanted[i], 0)], out_ref.at[i], sems.at[1]
        ).start()
        return carry

    lax.fori_loop(0, out_ref.shape[0], step, 0, unroll=8)
    pltpu.make_async_copy(out_ref, out_ref, sems.at[1]).wait()


def finish_kernel(part_ref, ret_in, ret_out, wide, sem):
    wide[...] = jnp.broadcast_to(part_ref[...][None], wide.shape)
    extra = wide.shape[1]
    rows = pl.ds(ret_out.shape[1] - extra, extra)
    copy = pltpu.make_async_copy(wide, ret_out.at[:, rows], sem)
    copy.start()
    copy.wait()


def combine_kernel(wanted, back_hbm, base_ref, out_hbm, grad_hbm, back, acc, grad, out, sems, ends):
    devices, lines, _ = back.shape
    groups = sems.shape[0]
    size = devices // groups
    width = base_ref.shape[-1]
    slots = width // LANES
    extra = lines - KEY_SEG * slots
    tall = size // slots * extra

    def copy(t):
        part = pl.ds(t * size, size)
        return pltpu.make_async_copy(back_hbm.at[part], back.at[part], sems.at[t])

    for t in range(groups):
        copy(t).start()
    acc[...] = base_ref[...]
    for t in range(groups):
        copy(t).wait()
        for i in range(t * size, (t + 1) * size):
            rows = pl.ds((i // slots) * extra, extra)
            cols = pl.ds((i % slots) * LANES, LANES)
            grad[rows, cols] = back[i, pl.ds(lines - extra, extra), :].astype(F32)
        part = pl.ds(t * tall, tall)
        pltpu.make_async_copy(grad.at[part], grad_hbm.at[part], ends.at[0]).start()

        def step(i, carry):
            seg = wanted[i]

            @pl.when(seg >= 0)
            def _():
                for u in range(slots):
                    cols = pl.ds(u * LANES, LANES)
                    acc[seg, :, cols] += back[i, pl.ds(u * KEY_SEG, KEY_SEG), :].astype(F32)

            return carry

        lax.fori_loop(t * size, (t + 1) * size, step, 0)
    out[...] = acc[...].astype(out.dtype)
    last = pltpu.make_async_copy(out, out_hbm, ends.at[1])
    last.start()
    pltpu.make_async_copy(grad, grad_hbm, ends.at[0]).wait()
    last.wait()


def exchange(v):
    return lax.all_to_all(v, AXES, split_axis=0, concat_axis=0, tiled=True)


def local(views_x, dy, w_query, w_key, w_value, w_out, key_lists, key_counts):
    width = views_x.shape[-1]
    x = views_x.reshape(-1, width)
    grads = dy.reshape(-1, width)
    tokens = x.shape[0]
    devices = lax.axis_size(AXES)
    me = lax.axis_index(AXES)
    seg_dev = tokens // KEY_SEG
    blocks = tokens // QUERY_BLOCK
    columns = jnp.arange(MAXK, dtype=jnp.int32)
    live = columns[None, :] < key_counts[:, None]
    asked = live & (key_lists // seg_dev == me)
    wanted = jnp.max(
        jnp.where(asked, key_lists % seg_dev, -1).reshape(devices, blocks * MAXK), axis=1
    )
    outgoing = pl.pallas_call(
        gather_kernel,
        out_shape=jax.ShapeDtypeStruct((devices, KEY_SEG, width), BF16),
        in_specs=[SMEM, ANY],
        out_specs=ANY,
        scratch_shapes=[
            pltpu.VMEM((seg_dev, KEY_SEG, width), BF16),
            pltpu.SemaphoreType.DMA((2,)),
        ],
        name="gather",
    )(wanted, x.reshape(seg_dev, KEY_SEG, width))
    fetched = exchange(outgoing)

    queries = dot(x, w_query).astype(BF16) * BF16(HEAD_DIM ** -0.5)
    grad_out = dot(grads, w_out, 1, 1).astype(BF16)
    queries_t = queries.T
    grad_out_t = grad_out.T
    mine = lax.dynamic_slice_in_dim(key_lists, me * blocks, blocks, 0)
    counts = lax.dynamic_slice_in_dim(key_counts, me * blocks, blocks, 0)
    sources = jnp.where(columns[None, :] < counts[:, None], mine // seg_dev, me).reshape(-1)
    entry = jnp.arange(blocks * MAXK, dtype=jnp.int32)
    same = sources[:, None] == sources[None, :]
    first = 1 - jnp.any(same & (entry[None, :] < entry[:, None]), axis=1).astype(jnp.int32)
    last = 1 - jnp.any(same & (entry[None, :] > entry[:, None]), axis=1).astype(jnp.int32)
    keys, values, stats, pieces = forward(
        sources, counts, fetched, queries_t, grad_out_t, w_key, w_value, grads
    )
    parts = exchange(pieces)
    ret, dq_t = backward(
        sources, counts, first, last, keys, values, queries, grad_out, queries_t, grad_out_t,
        stats, w_key.T, w_value.T, devices
    )
    part = jnp.sum(parts.astype(F32), axis=0).astype(BF16)
    ret = pl.pallas_call(
        finish_kernel,
        out_shape=jax.ShapeDtypeStruct(ret.shape, ret.dtype),
        in_specs=[VMEM, ANY],
        out_specs=ANY,
        scratch_shapes=[pltpu.VMEM(parts.shape, BF16), pltpu.SemaphoreType.DMA],
        input_output_aliases={1: 0},
        compiler_params=pltpu.CompilerParams(vmem_limit_bytes=57 * MIB),
        name="finish",
    )(part, ret)
    back = exchange(ret)
    base = dot(dq_t, w_query, 0, 1)
    grad_x, grad_w_out = pl.pallas_call(
        combine_kernel,
        out_shape=[
            jax.ShapeDtypeStruct((seg_dev, KEY_SEG, width), BF16),
            jax.ShapeDtypeStruct((width, width), F32),
        ],
        in_specs=[SMEM, ANY, VMEM],
        out_specs=[ANY, ANY],
        scratch_shapes=[
            pltpu.VMEM(ret.shape, BF16),
            pltpu.VMEM((seg_dev, KEY_SEG, width), F32),
            pltpu.VMEM((width, width), F32),
            pltpu.VMEM((seg_dev, KEY_SEG, width), BF16),
            pltpu.SemaphoreType.DMA((8,)),
            pltpu.SemaphoreType.DMA((2,)),
        ],
        compiler_params=pltpu.CompilerParams(vmem_limit_bytes=24 * MIB),
        name="combine",
    )(wanted, back, base.reshape(seg_dev, KEY_SEG, width))
    return grad_x.reshape(views_x.shape), grad_w_out


def solution(mesh):
    in_specs = (P("view", "row", None), P("view", "row", None), P(), P(), P(), P(), P(), P())
    out_specs = (P("view", "row", None), P())
    return jax.shard_map(local, mesh=mesh, in_specs=in_specs, out_specs=out_specs, check_vma=False)
```
